256 devices in a mesh: ctx: 32 (over z, x_lo, core), head: 8 (over x_hi, y).
Axes of the slice: x: 4 (x_hi: 2, x_lo: 2; x = x_hi * 2 + x_lo), y: 4, z: 8, core: 2. Of those that a mesh axis runs over, the one named last changes fastest.
Arguments:
- queries: bfloat16 [16384, 2048], P('ctx', 'head'), may hold values from -120 to 120
- keys: bfloat16 [16384, 2048], P('ctx', 'head'), may hold values from -5 to 5
- values: bfloat16 [16384, 2048], P('ctx', 'head'), may hold values from -5 to 5
- w_out: bfloat16 [2048, 4096], P('head'), may hold values from -0.1875 to 0.1875
Outputs:
- mixed: bfloat16 [16384, 4096], P('ctx', 'head')
The draws below stay inside these ranges and needn't reach their ends.
All inputs are finite; a program needn't handle non-finite values.
Results may differ from the reference program's by a relative error of at most 0.017.
Values may be sent and summed in bfloat16 or wider, within the bound.
No kernel may reach another device: no remote copies, remote signals or barrier semaphores. Data moves between devices by JAX's collectives and lax.ppermute only.
A program may use at most 128 MiB of HBM per device.

```python
import math
import jax
import jax.numpy as jnp
from jax import lax

D = 4096
HEADS = 16
HEAD = 128
TOKENS = 16384


def shared_base(key):
    return jnp.clip(jax.random.normal(key, (TOKENS, HEADS * HEAD), jnp.float32), -4.0, 4.0)


def draw_keys(key, part):
    base = shared_base(key)
    return base.astype(jnp.bfloat16)


def draw_queries(key, part):
    key = jax.random.fold_in(key, 22)
    return jnp.clip(jax.random.normal(key, (TOKENS, HEADS * HEAD), jnp.float32), -4.0, 4.0).astype(jnp.bfloat16)


def raised(result, stream_key, source, target, shards_of, factor):
    def block_of(axis_at):
        return (jnp.arange(result.shape[axis_at]) // (result.shape[axis_at] // shards_of)).reshape((-1,) + (1,) * (result.ndim - 1 - axis_at))

    first = jax.random.permutation(stream_key, shards_of)[block_of(target)]
    far = (block_of(target) + shards_of // 2) % shards_of
    return jnp.where((block_of(source) == first) | (block_of(source) == far), factor * result, result)


def shard_levels(key, shape, pieces, low, largest):
    level, own = 1.0, jax.random.fold_in(key, 6)
    for position, blocks in pieces:
        heights = jnp.exp(jax.random.uniform(jax.random.fold_in(own, position), (blocks,), jnp.float32, low / len(pieces), largest / len(pieces)))
        level = level * jnp.repeat(heights, shape[position] // blocks).reshape([-1 if axis == position else 1 for axis in range(len(shape))])
    return level


def centred(rng, dims, scale, limit, pieces=(), held_as=jnp.bfloat16):
    values = jax.random.normal(rng, dims, jnp.float32) * scale
    if len(pieces) > 0:
        values = shard_levels(rng, dims, pieces, -0.22, 0.18) * values
    return jnp.clip(values, min=-limit, max=limit).astype(held_as)


def gaussian_with(key, shape, deviation, reach, shards, heavy, kind=jnp.bfloat16):
    values = deviation * jax.random.normal(key, shape, jnp.float32)
    if shards:
        values = values * shard_levels(key, shape, shards, -0.22, 0.18)
    return jnp.clip(raised(values, jax.random.fold_in(key, 3), *heavy), -reach, reach).astype(kind)


def setup_inputs(seed: int = 0) -> dict:
    seeds = jax.random.split(jax.random.key(seed), 5)
    queries = draw_queries(jax.random.fold_in(seeds[4], 71), 0)
    keys = draw_keys(jax.random.fold_in(seeds[4], 71), 0)
    values = centred(seeds[2], (TOKENS, HEADS * HEAD), 1.0, 5.0, ((0, 32), (1, 8)))
    w_out = gaussian_with(seeds[3], (HEADS * HEAD, D), (HEADS * HEAD) ** -0.5, 0.1875, ((0, 8),), (0, 1, 8, 2.0))
    return {"queries": queries, "keys": keys, "values": values, "w_out": w_out}


def attend_block(query_block, keys_head, values_head, first_row):
    scale_factor = HEAD ** -0.5
    scores = jnp.dot(query_block, keys_head.T, preferred_element_type=jnp.float32) * scale_factor
    query_pos = first_row + jnp.arange(query_block.shape[0], dtype=jnp.int32)
    key_pos = jnp.arange(keys_head.shape[0], dtype=jnp.int32)
    allowed = key_pos[None, :] <= query_pos[:, None]
    scores = jnp.where(allowed, scores, jnp.float32(-1e30))
    row_top = jnp.max(scores, axis=1)
    weights = jnp.where(allowed, jnp.exp(scores - row_top[:, None]), jnp.float32(0.0))
    row_total = jnp.sum(weights, axis=1)
    summed = jnp.dot(weights.astype(jnp.bfloat16), values_head, preferred_element_type=jnp.float32)
    return (summed / row_total[:, None]).astype(jnp.bfloat16)


def reference(queries, keys, values, w_out):
    block_rows = math.gcd(TOKENS, 1024)
    query_heads = queries.reshape(TOKENS, HEADS, HEAD).transpose(1, 0, 2)
    key_heads = keys.reshape(TOKENS, HEADS, HEAD).transpose(1, 0, 2)
    value_heads = values.reshape(TOKENS, HEADS, HEAD).transpose(1, 0, 2)
    outputs = []
    for block_index in range(TOKENS // block_rows):
        first_row = block_index * block_rows
        last_row = first_row + block_rows

        def per_head(triple):
            return attend_block(triple[0], triple[1], triple[2], first_row)

        outputs.append(lax.map(per_head, (query_heads[:, first_row:last_row], key_heads[:, :last_row], value_heads[:, :last_row])))
    attended = jnp.concatenate(outputs, axis=1).transpose(1, 0, 2).reshape(TOKENS, HEADS * HEAD)
    return jnp.dot(attended, w_out, preferred_element_type=jnp.float32).astype(jnp.bfloat16)
```

```python
import functools

import jax
import jax.numpy as jnp
from jax import lax
from jax.experimental import pallas as pl
from jax.experimental.pallas import tpu as pltpu
from jax.sharding import Mesh, PartitionSpec as P

HEAD = 128
ROWS = 512
SUB = 256
PAY = HEAD + 16
LOG2E = 1.4426950408889634
SCALE = HEAD ** (-0.5) * LOG2E
LOW = -1e30
BF = jnp.bfloat16
F32 = jnp.float32
VMEM = pl.BlockSpec(memory_space=pltpu.VMEM)
SMEM = pl.BlockSpec(memory_space=pltpu.SMEM)
PARAMS = pltpu.CompilerParams(vmem_limit_bytes=40 * 1024 * 1024)


def call(kernel, shapes, operands, scratch=(), flops=0, bytes_accessed=0, exps=0, smem=0):
    return pl.pallas_call(
        kernel,
        out_shape=shapes,
        in_specs=[SMEM] * smem + [VMEM] * (len(operands) - smem),
        out_specs=jax.tree.map(lambda _: VMEM, shapes),
        scratch_shapes=scratch,
        compiler_params=PARAMS,
        cost_estimate=pl.CostEstimate(flops=flops, bytes_accessed=bytes_accessed, transcendentals=exps),
    )(*operands)


def prepare(q_ref, k_ref, v_ref, qt_ref, kv0_ref, kv1_ref):
    qt_ref[...] = q_ref[...].T
    for head, out in ((0, kv0_ref), (1, kv1_ref)):
        columns = slice(head * HEAD, (head + 1) * HEAD)
        out[0:ROWS, :] = k_ref[:, columns]
        for block in range(ROWS // HEAD):
            rows = slice(block * HEAD, (block + 1) * HEAD)
            out[ROWS + block * HEAD : ROWS + (block + 1) * HEAD, :] = v_ref[rows, columns].T


def attend(head, where_ref, q0, q1, q2, q3, kv_ref, o0, o1, o2, o3, m_ref, l_ref, acc_ref):
    plane, place = where_ref[0], where_ref[1]
    queries = (q0, q1, q2, q3)
    outs = (o0, o1, o2, o3)
    m_ref[...] = jnp.full(m_ref.shape, LOW, F32)
    l_ref[...] = jnp.zeros(l_ref.shape, F32)
    acc_ref[...] = jnp.zeros(acc_ref.shape, F32)

    def chunk(index):
        keys = kv_ref[index, 0:ROWS, :]
        blocks = [
            kv_ref[index, ROWS + b * HEAD : ROWS + (b + 1) * HEAD, :] for b in range(ROWS // HEAD)
        ]
        return keys, jnp.concatenate(blocks, axis=1)

    def absorb(piece, keys, values, masked):
        for sub in range(ROWS // SUB):
            columns = slice(piece * ROWS + sub * SUB, piece * ROWS + (sub + 1) * SUB)
            qt = queries[piece][head * HEAD : (head + 1) * HEAD, sub * SUB : (sub + 1) * SUB]
            scores = jnp.dot(keys, qt, preferred_element_type=F32) * SCALE
            if masked:
                key_at = lax.broadcasted_iota(jnp.int32, scores.shape, 0)
                query_at = lax.broadcasted_iota(jnp.int32, scores.shape, 1) + sub * SUB
                scores = jnp.where(key_at <= query_at, scores, LOW)
            old = m_ref[:, columns]
            new = jnp.maximum(old, jnp.max(scores, axis=0, keepdims=True))
            weights = jnp.exp2(scores - new)
            fade = jnp.exp2(old - new)
            m_ref[:, columns] = new
            l_ref[:, columns] = l_ref[:, columns] * fade + jnp.sum(weights, axis=0, keepdims=True)
            acc_ref[:, columns] = acc_ref[:, columns] * fade + jnp.dot(
                values, weights.astype(BF), preferred_element_type=F32
            )

    keys, values = chunk(plane)
    absorb(0, keys, values, True)
    for piece in range(1, 4):
        pl.when((place ^ piece) > place)(functools.partial(absorb, piece, keys, values, False))

    def step(index, carry):
        keys, values = chunk(index)
        for piece in range(4):
            absorb(piece, keys, values, False)
        return carry

    lax.fori_loop(0, plane, step, 0)
    for piece in range(4):
        columns = slice(piece * ROWS, (piece + 1) * ROWS)
        total = l_ref[:, columns]
        some = total > 0.0
        safe = jnp.where(some, total, 1.0)
        outs[piece][0:HEAD, :] = (acc_ref[:, columns] / safe).astype(BF)
        level = jnp.where(some, m_ref[:, columns] + jnp.log2(safe), LOW)
        high = level.astype(BF)
        rest = level - high.astype(F32)
        middle = rest.astype(BF)
        low = (rest - middle.astype(F32)).astype(BF)
        row = lax.broadcasted_iota(jnp.int32, (16, ROWS), 0)
        parts = jnp.where(
            row == 0,
            high.astype(F32),
            jnp.where(row == 1, middle.astype(F32), jnp.where(row == 2, low.astype(F32), 0.0)),
        )
        outs[piece][HEAD:PAY, :] = parts.astype(BF)


def merge(p0, p1, p2, p3, out_ref):
    pieces = (p0, p1, p2, p3)
    levels = []
    for piece in pieces:
        parts = piece[HEAD:PAY, :].astype(F32)
        levels.append(parts[0:1, :] + parts[1:2, :] + parts[2:3, :])
    top = functools.reduce(jnp.maximum, levels)
    shares = [jnp.exp2(level - top) for level in levels]
    total = functools.reduce(jnp.add, shares)
    mixed = sum(
        piece[0:HEAD, :].astype(F32) * (share / total) for piece, share in zip(pieces, shares)
    )
    out_ref[...] = mixed.T.astype(BF)


def project(head, count, *refs):
    terms, weights = refs[:count], refs[count : 2 * count]
    out_ref = refs[-1]
    total = refs[2 * count][...] if len(refs) > 2 * count + 1 else None
    for at in range(0, count, 2):
        left = jnp.concatenate([terms[at][...], terms[at + 1][...]], axis=1)
        rows = slice(head * HEAD, (head + 1) * HEAD)
        right = jnp.concatenate([weights[at][rows, :], weights[at + 1][rows, :]], axis=0)
        term = jnp.dot(left, right, preferred_element_type=F32)
        total = term if total is None else total + term
    out_ref[...] = total.astype(out_ref.dtype)


def turn(value, axis, size, step):
    return lax.ppermute(value, axis, [(i, (i + step) % size) for i in range(size)])


def local(queries, keys, values, w_out):
    plane = lax.axis_index("z")
    place = lax.axis_index("xl") * 2 + lax.axis_index("c")
    where = jnp.stack([plane, place]).astype(jnp.int32)
    qt, kv0, kv1 = call(
        prepare,
        (
            jax.ShapeDtypeStruct((2 * HEAD, ROWS), BF),
            jax.ShapeDtypeStruct((2 * ROWS, HEAD), BF),
            jax.ShapeDtypeStruct((2 * ROWS, HEAD), BF),
        ),
        (queries, keys, values),
        bytes_accessed=3 * 2**19,
    )
    gathered = [lax.all_gather(kv, "z", axis=0) for kv in (kv0, kv1)]
    swap4 = lambda v, e: lax.ppermute(v, ("xl", "c"), [(i, i ^ e) for i in range(4)])
    q_pieces = [qt] + [swap4(qt, e) for e in (1, 2, 3)]

    xh, y = lax.axis_index("xh"), lax.axis_index("y")
    w_pieces = []
    for dx in (0, 1):
        for dy in (0, 1, 3, 2):
            to = (xh ^ dx) * 4 + (y - dy) % 4
            part = lax.dynamic_slice(w_out, (0, to * ROWS), (2 * HEAD, ROWS))
            if dx or dy:
                pairs = [
                    (a * 4 + b, (a ^ dx) * 4 + (b - dy) % 4) for a in range(2) for b in range(4)
                ]
                part = lax.ppermute(part, ("xh", "y"), pairs)
            w_pieces.append(part)

    total = None
    for head in range(2):
        payload = call(
            functools.partial(attend, head),
            tuple(jax.ShapeDtypeStruct((PAY, ROWS), BF) for _ in range(4)),
            (where, *q_pieces, gathered[head]),
            scratch=(
                pltpu.VMEM((1, 4 * ROWS), F32),
                pltpu.VMEM((1, 4 * ROWS), F32),
                pltpu.VMEM((HEAD, 4 * ROWS), F32),
            ),
            flops=8 * 2**29,
            bytes_accessed=4 * 2**20,
            exps=8 * 2**20,
            smem=1,
        )
        received = [payload[0]] + [swap4(payload[e], e) for e in (1, 2, 3)]
        own = call(merge, jax.ShapeDtypeStruct((ROWS, HEAD), BF), tuple(received), bytes_accessed=2**20)
        terms = []
        for half in (own, turn(own, "xh", 2, 1)):
            terms += [half, turn(half, "y", 4, -1), turn(half, "y", 4, 1), turn(half, "y", 4, 2)]
        operands = (*terms, *w_pieces) + (() if total is None else (total,))
        total = call(
            functools.partial(project, head, 8),
            jax.ShapeDtypeStruct((ROWS, ROWS), F32 if head == 0 else BF),
            operands,
            flops=2 * ROWS * ROWS * 1024,
            bytes_accessed=4 * 2**20,
        )
    return total


def solution(mesh):
    fine = Mesh(mesh.devices.reshape(8, 2, 2, 2, 4), ("z", "xl", "c", "xh", "y"))
    ctx, head = ("z", "xl", "c"), ("xh", "y")
    in_specs = (P(ctx, head), P(ctx, head), P(ctx, head), P(head, None))
    return jax.shard_map(
        local, mesh=fine, in_specs=in_specs, out_specs=P(ctx, head), check_vma=False
    )
```

```python
import functools

import jax
import jax.numpy as jnp
from jax import lax
from jax.experimental import pallas as pl
from jax.experimental.pallas import tpu as pltpu
from jax.sharding import Mesh, PartitionSpec as P

HEAD = 128
ROWS = 512
HALF = 256
REACH = 100.0
PAY = HEAD + 16
LOG2E = 1.4426950408889634
SCALE = HEAD ** (-0.5) * LOG2E
LOW = -1e30
BF = jnp.bfloat16
F32 = jnp.float32
VMEM = pl.BlockSpec(memory_space=pltpu.VMEM)
HBM = pl.BlockSpec(memory_space=pl.ANY)
SMEM = pl.BlockSpec(memory_space=pltpu.SMEM)
PARAMS = pltpu.CompilerParams(vmem_limit_bytes=24 * 1024 * 1024)
LARGE = pltpu.CompilerParams(vmem_limit_bytes=8 * 1024 * 1024)
SMALL = pltpu.CompilerParams(vmem_limit_bytes=8 * 1024 * 1024)


def call(kernel, shapes, operands, scratch=(), flops=0, bytes_accessed=0, exps=0, smem=0, far=0, aliases=None):
    return pl.pallas_call(
        kernel,
        out_shape=shapes,
        in_specs=[SMEM] * smem + [VMEM] * (len(operands) - smem - far) + [HBM] * far,
        out_specs=jax.tree.map(lambda _: VMEM, shapes),
        scratch_shapes=scratch,
        input_output_aliases=aliases or {},
        compiler_params=PARAMS,
        cost_estimate=pl.CostEstimate(flops=flops, bytes_accessed=bytes_accessed, transcendentals=exps),
    )(*operands)


def prepare(q_far, k_far, v_far, qt0_ref, qt1_ref, kv0_ref, kv1_ref, q_ref, k_ref, v_ref, sem):
    copies = [
        pltpu.make_async_copy(far, near, sem.at[at])
        for at, (far, near) in enumerate(((q_far, q_ref), (k_far, k_ref), (v_far, v_ref)))
    ]
    for copy in copies:
        copy.start()
    for copy in copies:
        copy.wait()
    turned = q_ref[...].T
    qt0_ref[...] = turned[0:HEAD, :]
    qt1_ref[...] = turned[HEAD : 2 * HEAD, :]
    for head, out in ((0, kv0_ref), (1, kv1_ref)):
        columns = slice(head * HEAD, (head + 1) * HEAD)
        for half in range(2):
            at = half * ROWS
            out[at : at + HALF, :] = k_ref[half * HALF : (half + 1) * HALF, columns]
            for block in range(2):
                rows = slice(half * HALF + block * HEAD, half * HALF + (block + 1) * HEAD)
                to = at + HALF + block * HEAD
                out[to : to + HEAD, :] = v_ref[rows, columns].T


def unpack(first, second):
    keys = jnp.concatenate([first[0:HALF, :], second[0:HALF, :]], axis=0)
    blocks = [part[HALF + b * HEAD : HALF + (b + 1) * HEAD, :] for part in (first, second) for b in (0, 1)]
    return keys, jnp.concatenate(blocks, axis=1)


def spot():
    return lax.axis_index("xl") * 2 + lax.axis_index("c")


class Flash:
    def __init__(self, place, queries, stat_ref, acc_ref, query_ref):
        self.place, self.query_ref = place, query_ref
        for piece, query in enumerate(queries):
            query_ref[:, self.columns(piece)] = query[...]
        self.stat_ref, self.acc_ref = stat_ref, acc_ref

    def columns(self, piece):
        if isinstance(piece, int):
            return slice(piece * ROWS, (piece + 1) * ROWS)
        return pl.ds(pl.multiple_of(piece * ROWS, ROWS), ROWS)

    def query(self, piece):
        return self.query_ref[:, self.columns(piece)]

    def start(self):
        width = 4 * ROWS
        self.stat_ref[0:1, :] = jnp.full((1, width), LOW, F32)
        self.stat_ref[1:2, :] = jnp.zeros((1, width), F32)
        self.acc_ref[...] = jnp.zeros(self.acc_ref.shape, F32)
        query = self.query_ref[...].astype(F32)
        self.stat_ref[2:3, :] = jnp.sqrt(jnp.sum(query * query, axis=0, keepdims=True)) * SCALE

    def score(self, piece, keys):
        return jnp.dot(keys, self.query(piece), preferred_element_type=F32) * SCALE

    def settle(self, piece, scores):
        columns = self.columns(piece)
        old = self.stat_ref[0:1, columns]
        new = jnp.maximum(old, jnp.max(scores, axis=0, keepdims=True))
        weights = jnp.exp2(scores - new)
        fade = jnp.exp2(old - new)
        self.stat_ref[0:1, columns] = new
        self.stat_ref[1:2, columns] = self.stat_ref[1:2, columns] * fade + jnp.sum(
            weights, axis=0, keepdims=True
        )
        self.acc_ref[:, columns] = self.acc_ref[:, columns] * fade
        return weights.astype(BF)

    def keep(self, piece, scores):
        columns = self.columns(piece)
        weights = jnp.exp2(scores - self.stat_ref[0:1, columns])
        self.stat_ref[1:2, columns] = self.stat_ref[1:2, columns] + jnp.sum(
            weights, axis=0, keepdims=True
        )
        return weights.astype(BF)

    def gather(self, piece, values, weights):
        columns = self.columns(piece)
        self.acc_ref[:, columns] = self.acc_ref[:, columns] + jnp.dot(
            values, weights, preferred_element_type=F32
        )

    def absorb(self, keys, values):
        following, waiting = self.score(0, keys), None
        for piece in range(4):
            scores = following
            if piece < 3:
                following = self.score(piece + 1, keys)
            if waiting is not None:
                self.gather(*waiting)
            waiting = (piece, values, self.keep(piece, scores))
        self.gather(*waiting)

    def level(self, piece, keys, values):
        self.gather(piece, values, self.settle(piece, self.score(piece, keys)))

    def full(self, keys, values):
        sizes = keys.astype(F32)
        longest = jnp.max(jnp.sum(sizes * sizes, axis=1, keepdims=True))
        reach = jnp.max(self.stat_ref[2:3, :]) ** 2 * longest
        lowest = jnp.min(self.stat_ref[0:1, :])
        room = lowest + REACH
        stays = (room > 0.0) & (reach <= room * room)

        @pl.when(stays)
        def _():
            self.absorb(keys, values)

        @pl.when(jnp.logical_not(stays))
        def _():
            @pl.loop(0, 4)
            def _(piece):
                self.level(piece, keys, values)

    def diagonal(self, keys, values):
        scores = self.score(0, keys)
        key_at = lax.broadcasted_iota(jnp.int32, scores.shape, 0)
        query_at = lax.broadcasted_iota(jnp.int32, scores.shape, 1)
        scores = jnp.where(key_at <= query_at, scores, LOW)
        self.gather(0, values, self.settle(0, scores))
        @pl.loop(1, 4)
        def _(piece):
            @pl.when((self.place ^ piece) > self.place)
            def _():
                self.level(piece, keys, values)

    def finish(self, outs):
        for piece in range(4):
            columns = self.columns(piece)
            total = self.stat_ref[1:2, columns]
            some = total > 0.0
            safe = jnp.where(some, total, 1.0)
            outs[piece][0:HEAD, :] = (self.acc_ref[:, columns] / safe).astype(BF)
            level = jnp.where(some, self.stat_ref[0:1, columns] + jnp.log2(safe), LOW)
            high = level.astype(BF)
            rest = level - high.astype(F32)
            middle = rest.astype(BF)
            low = (rest - middle.astype(F32)).astype(BF)
            row = lax.broadcasted_iota(jnp.int32, (16, ROWS), 0)
            parts = jnp.where(
                row == 0,
                high.astype(F32),
                jnp.where(row == 1, middle.astype(F32), jnp.where(row == 2, low.astype(F32), 0.0)),
            )
            outs[piece][HEAD:PAY, :] = parts.astype(BF)


def attend_whole(q0, q1, q2, q3, kv_ref, _, o0, o1, o2, o3, stat_ref, acc_ref, query_ref, kv_all, sem):
    plane = lax.axis_index("z")
    flash = Flash(spot(), (q0, q1, q2, q3), stat_ref, acc_ref, query_ref)

    def fetch(index):
        return pltpu.make_async_copy(kv_ref.at[index], kv_all.at[index], sem.at[index])

    def chunk(index):
        fetch(index).wait()
        return unpack(kv_all[index, 0:ROWS, :], kv_all[index, ROWS : 2 * ROWS, :])

    lax.fori_loop(0, 8, lambda index, carry: fetch(index).start() or carry, 0)
    flash.start()
    flash.diagonal(*chunk(plane))
    lax.fori_loop(0, plane, lambda index, carry: flash.full(*chunk(index)) or carry, 0)
    lax.fori_loop(plane + 1, 8, lambda index, carry: fetch(index).wait() or carry, 0)
    flash.finish((o0, o1, o2, o3))


def attend_first(q0, q1, q2, q3, own, up, down, stat_ref, acc_ref, query_ref, chunk_ref):
    plane = lax.axis_index("z")
    flash = Flash(spot(), (q0, q1, q2, q3), stat_ref, acc_ref, query_ref)
    flash.start()
    flash.diagonal(*unpack(own[0:ROWS, :], own[ROWS : 2 * ROWS, :]))
    either(flash, plane, 1, up, down, chunk_ref)


def either(flash, plane, distance, up, down, chunk_ref):
    @pl.loop(0, 2)
    def _(side):
        for at, active, part in ((0, plane >= distance, up), (1, plane + distance >= 8, down)):

            @pl.when(active & (side == at))
            def _():
                chunk_ref[...] = part[...]

        @pl.when(jnp.where(side == 0, plane >= distance, plane + distance >= 8))
        def _():
            flash.full(*unpack(chunk_ref[0:ROWS, :], chunk_ref[ROWS : 2 * ROWS, :]))


def attend_next(distance, q0, q1, q2, q3, up, down, stat_in, acc_in, stat_ref, acc_ref, query_ref, chunk_ref):
    stat_ref[...] = stat_in[...]
    acc_ref[...] = acc_in[...]
    flash = Flash(spot(), (q0, q1, q2, q3), stat_ref, acc_ref, query_ref)
    either(flash, lax.axis_index("z"), distance, up, down, chunk_ref)


def attend_last(q0, q1, q2, q3, up, down, stat_in, acc_in, o0, o1, o2, o3, stat_ref, acc_ref, query_ref):
    stat_ref[...] = stat_in[...]
    acc_ref[...] = acc_in[...]
    flash = Flash(spot(), (q0, q1, q2, q3), stat_ref, acc_ref, query_ref)

    @pl.when(lax.axis_index("z") >= 4)
    def _():
        flash.full(*unpack(up[...], down[...]))

    flash.finish((o0, o1, o2, o3))


def merge(p0, p1, p2, p3, *others):
    out_ref = others[-1]
    pieces = (p0, p1, p2, p3)
    levels = []
    for piece in pieces:
        parts = piece[HEAD:PAY, :].astype(F32)
        levels.append(parts[0:1, :] + parts[1:2, :] + parts[2:3, :])
    top = functools.reduce(jnp.maximum, levels)
    shares = [jnp.exp2(level - top) for level in levels]
    total = functools.reduce(jnp.add, shares)
    mixed = sum(
        piece[0:HEAD, :].astype(F32) * (share / total) for piece, share in zip(pieces, shares)
    )
    out_ref[...] = mixed.T.astype(BF)


def project(*refs):
    near, far, weight, out_ref = refs[:8], refs[8:16], refs[16], refs[17]
    total = None
    for at in range(8):
        left = jnp.concatenate([near[at][...], far[at][...]], axis=1)
        term = jnp.dot(left, weight[at], preferred_element_type=F32)
        total = term if total is None else total + term
    out_ref[...] = total.astype(out_ref.dtype)


def hold(values, *after):
    count = len(values)
    return pl.pallas_call(
        lambda *refs: None,
        out_shape=tuple(jax.ShapeDtypeStruct(v.shape, v.dtype) for v in values),
        in_specs=[HBM] * (count + len(after)),
        out_specs=(HBM,) * count,
        input_output_aliases={i: i for i in range(count)},
        compiler_params=SMALL,
    )(*values, *after)


def turn(value, axis, size, step):
    return lax.ppermute(value, axis, [(i, (i + step) % size) for i in range(size)])


def around(own):
    return [
        part
        for half in (own, turn(own, "xh", 2, 1))
        for part in (half, turn(half, "y", 4, -1), turn(half, "y", 4, 1), turn(half, "y", 4, 2))
    ]


def cut(w_far, _, mine, other, strip, sem):
    first = (lax.axis_index("z") * 2 + lax.axis_index("c")) * 16
    copy = pltpu.make_async_copy(w_far.at[pl.ds(pl.multiple_of(first, 16), 16), :], strip, sem)
    copy.start()
    copy.wait()
    for out, side in ((mine, lax.axis_index("xh")), (other, lax.axis_index("xh") ^ 1)):
        out[...] = strip[:, pl.ds(pl.multiple_of(side * (4 * ROWS), 4 * ROWS), 4 * ROWS)]


def split(mine, other, _, *outs):
    for out, dy in zip(outs, (0, 1, 3, 2)):
        columns = pl.ds(pl.multiple_of(((lax.axis_index("y") + 4 - dy) & 3) * ROWS, ROWS), ROWS)
        out[0:16, :] = mine[:, columns]
        out[16:32, :] = other[:, columns]


def pile(*refs):
    for at in range(8):
        refs[4][at] = refs[at % 4][(at // 4) * 16 : (at // 4) * 16 + 16, :]


def halve(up, down, first, second):
    first[...] = up[0:ROWS, :]
    second[...] = down[ROWS : 2 * ROWS, :]


def swap4(value, e):
    return lax.ppermute(value, ("xl", "c"), [(i, i ^ e) for i in range(4)])


def local(queries, keys, values, w_out):
    qt0, qt1, kv0, kv1 = pl.pallas_call(
        prepare,
        out_shape=(
            jax.ShapeDtypeStruct((HEAD, ROWS), BF),
            jax.ShapeDtypeStruct((HEAD, ROWS), BF),
            jax.ShapeDtypeStruct((2 * ROWS, HEAD), BF),
            jax.ShapeDtypeStruct((2 * ROWS, HEAD), BF),
        ),
        in_specs=[HBM] * 3,
        out_specs=(VMEM,) * 4,
        scratch_shapes=(*[pltpu.VMEM((ROWS, 2 * HEAD), BF)] * 3, pltpu.SemaphoreType.DMA((3,))),
        compiler_params=LARGE,
        cost_estimate=pl.CostEstimate(flops=0, bytes_accessed=3 * 2**19, transcendentals=0),
    )(queries, keys, values)
    gathered = lax.all_gather(kv1, "z", axis=0)

    state_shapes = (jax.ShapeDtypeStruct((8, 4 * ROWS), F32), jax.ShapeDtypeStruct((HEAD, 4 * ROWS), F32))
    state_scratch = (pltpu.VMEM((8, 4 * ROWS), F32), pltpu.VMEM((HEAD, 4 * ROWS), F32))
    pay_shapes = tuple(jax.ShapeDtypeStruct((PAY, ROWS), BF) for _ in range(4))
    query_scratch = (pltpu.VMEM((HEAD, 4 * ROWS), BF),)
    chunk_scratch = (*query_scratch, pltpu.VMEM((2 * ROWS, HEAD), BF))
    costs = dict(flops=2**30, bytes_accessed=2**21, exps=2**21)

    up, down = turn(kv0, "z", 8, 1), turn(kv0, "z", 8, -1)
    q_pieces = [qt0] + [swap4(qt0, e) for e in (1, 2, 3)]
    up, down = hold((up, down), *q_pieces[1:])
    state = call(attend_first, state_shapes, (*q_pieces, kv0, up, down), scratch=chunk_scratch, **costs)
    (qt1,) = hold((qt1,), state[0])
    q_pieces1 = [qt1] + [swap4(qt1, e) for e in (1, 2, 3)]
    mine, other = call(
        cut,
        (jax.ShapeDtypeStruct((16, 4 * ROWS), BF),) * 2,
        (w_out, state[0]),
        scratch=(pltpu.VMEM((16, 8 * ROWS), BF), pltpu.SemaphoreType.DMA),
        far=2,
    )
    other = turn(other, "xh", 2, 1)
    for distance in (2, 3):
        up, down = turn(up, "z", 8, 1), turn(down, "z", 8, -1)
        up, down = hold((up, down), state[0], *(q_pieces1[1:] + [other] if distance == 2 else ()))
        state = call(
            functools.partial(attend_next, distance),
            state_shapes,
            (*q_pieces, up, down, *state),
            scratch=chunk_scratch,
            aliases={6: 0, 7: 1},
            **costs,
        )
    halves = call(halve, (jax.ShapeDtypeStruct((ROWS, HEAD), BF),) * 2, (up, down))
    strips = call(split, (jax.ShapeDtypeStruct((32, ROWS), BF),) * 4, (mine, other, up), far=1)
    strips = [strips[0]] + [turn(strip, "y", 4, -dy) for strip, dy in zip(strips[1:], (1, 3, 2))]
    last = (turn(halves[0], "z", 8, 1), turn(halves[1], "z", 8, -1))
    payload = call(attend_last, pay_shapes, (*q_pieces, *last, *state), scratch=(*state_scratch, *query_scratch), **costs)
    received = [payload[0]] + [swap4(payload[e], e) for e in (1, 2, 3)]
    early = received
    strip = call(pile, jax.ShapeDtypeStruct((8, 16, ROWS), BF), tuple(strips))
    weight = lax.all_gather(strip, ("z", "c"), axis=1, tiled=True)

    payload = call(
        attend_whole,
        pay_shapes,
        (*q_pieces1, gathered, early[1]),
        scratch=(*state_scratch, *query_scratch, pltpu.VMEM((8, 2 * ROWS, HEAD), BF), pltpu.SemaphoreType.DMA((8,))),
        flops=2**32,
        bytes_accessed=4 * 2**20,
        exps=8 * 2**20,
        far=2,
    )
    received = [payload[0]] + [swap4(payload[e], e) for e in (1, 2, 3)]
    own = call(merge, jax.ShapeDtypeStruct((ROWS, HEAD), BF), (*early, payload[0]), far=1)
    near = around(own)
    own = call(merge, jax.ShapeDtypeStruct((ROWS, HEAD), BF), (*received, near[4]), far=1)
    return call(
        project,
        jax.ShapeDtypeStruct((ROWS, ROWS), BF),
        (*near, *around(own), weight),
        flops=2**30,
        bytes_accessed=6 * 2**20,
    )


def solution(mesh):
    fine = Mesh(mesh.devices.reshape(8, 2, 2, 2, 4), ("z", "xl", "c", "xh", "y"))
    ctx, head = ("z", "xl", "c"), ("xh", "y")
    in_specs = (P(ctx, head), P(ctx, head), P(ctx, head), P(head, None))
    return jax.shard_map(
        local, mesh=fine, in_specs=in_specs, out_specs=P(ctx, head), check_vma=False
    )
```

```python
import functools

import jax
import jax.numpy as jnp
from jax import lax
from jax.experimental import pallas as pl
from jax.experimental.pallas import tpu as pltpu
from jax.sharding import Mesh, PartitionSpec as P

HEAD = 128
ROWS = 512
HALF = 256
REACH = 100.0
PAY = HEAD + 16
LOG2E = 1.4426950408889634
SCALE = HEAD ** (-0.5) * LOG2E
LOW = -1e30
BF = jnp.bfloat16
F32 = jnp.float32
VMEM = pl.BlockSpec(memory_space=pltpu.VMEM)
HBM = pl.BlockSpec(memory_space=pl.ANY)
SMEM = pl.BlockSpec(memory_space=pltpu.SMEM)
PARAMS = pltpu.CompilerParams(vmem_limit_bytes=24 * 1024 * 1024)
LARGE = pltpu.CompilerParams(vmem_limit_bytes=8 * 1024 * 1024)
SMALL = pltpu.CompilerParams(vmem_limit_bytes=8 * 1024 * 1024)


def call(kernel, shapes, operands, scratch=(), flops=0, bytes_accessed=0, exps=0, smem=0, far=0, aliases=None):
    return pl.pallas_call(
        kernel,
        out_shape=shapes,
        in_specs=[SMEM] * smem + [VMEM] * (len(operands) - smem - far) + [HBM] * far,
        out_specs=jax.tree.map(lambda _: VMEM, shapes),
        scratch_shapes=scratch,
        input_output_aliases=aliases or {},
        compiler_params=PARAMS,
        cost_estimate=pl.CostEstimate(flops=flops, bytes_accessed=bytes_accessed, transcendentals=exps),
    )(*operands)


def prepare(q_far, k_far, v_far, qt_ref, kv0_ref, kv1_ref, q_ref, k_ref, v_ref, sem):
    copies = [
        pltpu.make_async_copy(far, near, sem.at[at])
        for at, (far, near) in enumerate(((q_far, q_ref), (k_far, k_ref), (v_far, v_ref)))
    ]
    for copy in copies:
        copy.start()
    for copy in copies:
        copy.wait()
    turned = q_ref[...].T
    qt_ref[...] = turned
    for head, out in ((0, kv0_ref), (1, kv1_ref)):
        columns = slice(head * HEAD, (head + 1) * HEAD)
        for half in range(2):
            at = half * ROWS
            out[at : at + HALF, :] = k_ref[half * HALF : (half + 1) * HALF, columns]
            for block in range(2):
                rows = slice(half * HALF + block * HEAD, half * HALF + (block + 1) * HEAD)
                to = at + HALF + block * HEAD
                out[to : to + HEAD, :] = v_ref[rows, columns].T


def unpack(first, second):
    keys = jnp.concatenate([first[0:HALF, :], second[0:HALF, :]], axis=0)
    blocks = [part[HALF + b * HEAD : HALF + (b + 1) * HEAD, :] for part in (first, second) for b in (0, 1)]
    return keys, jnp.concatenate(blocks, axis=1)


def spot():
    return lax.axis_index("xl") * 2 + lax.axis_index("c")


class Flash:
    def __init__(self, head, place, queries, stat_ref, acc_ref, query_ref):
        self.place, self.query_ref = place, query_ref
        for piece, query in enumerate(queries):
            query_ref[:, self.columns(piece)] = query[head * HEAD : (head + 1) * HEAD, :]
        self.stat_ref, self.acc_ref = stat_ref, acc_ref

    def columns(self, piece):
        if isinstance(piece, int):
            return slice(piece * ROWS, (piece + 1) * ROWS)
        return pl.ds(pl.multiple_of(piece * ROWS, ROWS), ROWS)

    def query(self, piece):
        return self.query_ref[:, self.columns(piece)]

    def start(self):
        width = 4 * ROWS
        self.stat_ref[0:1, :] = jnp.full((1, width), LOW, F32)
        self.stat_ref[1:2, :] = jnp.zeros((1, width), F32)
        self.acc_ref[...] = jnp.zeros(self.acc_ref.shape, F32)
        query = self.query_ref[...].astype(F32)
        self.stat_ref[2:3, :] = jnp.sqrt(jnp.sum(query * query, axis=0, keepdims=True)) * SCALE

    def score(self, piece, keys):
        return jnp.dot(keys, self.query(piece), preferred_element_type=F32) * SCALE

    def settle(self, piece, scores):
        columns = self.columns(piece)
        old = self.stat_ref[0:1, columns]
        new = jnp.maximum(old, jnp.max(scores, axis=0, keepdims=True))
        weights = jnp.exp2(scores - new)
        fade = jnp.exp2(old - new)
        self.stat_ref[0:1, columns] = new
        self.stat_ref[1:2, columns] = self.stat_ref[1:2, columns] * fade + jnp.sum(
            weights, axis=0, keepdims=True
        )
        self.acc_ref[:, columns] = self.acc_ref[:, columns] * fade
        return weights.astype(BF)

    def keep(self, piece, scores):
        columns = self.columns(piece)
        weights = jnp.exp2(scores - self.stat_ref[0:1, columns])
        self.stat_ref[1:2, columns] = self.stat_ref[1:2, columns] + jnp.sum(
            weights, axis=0, keepdims=True
        )
        return weights.astype(BF)

    def gather(self, piece, values, weights):
        columns = self.columns(piece)
        self.acc_ref[:, columns] = self.acc_ref[:, columns] + jnp.dot(
            values, weights, preferred_element_type=F32
        )

    def absorb(self, keys, values):
        following, waiting = self.score(0, keys), None
        for piece in range(4):
            scores = following
            if piece < 3:
                following = self.score(piece + 1, keys)
            if waiting is not None:
                self.gather(*waiting)
            waiting = (piece, values, self.keep(piece, scores))
        self.gather(*waiting)

    def level(self, piece, keys, values):
        self.gather(piece, values, self.settle(piece, self.score(piece, keys)))

    def full(self, keys, values):
        sizes = keys.astype(F32)
        longest = jnp.max(jnp.sum(sizes * sizes, axis=1, keepdims=True))
        reach = jnp.max(self.stat_ref[2:3, :]) ** 2 * longest
        lowest = jnp.min(self.stat_ref[0:1, :])
        room = lowest + REACH
        stays = (room > 0.0) & (reach <= room * room)

        @pl.when(stays)
        def _():
            self.absorb(keys, values)

        @pl.when(jnp.logical_not(stays))
        def _():
            @pl.loop(0, 4)
            def _(piece):
                self.level(piece, keys, values)

    def diagonal(self, keys, values):
        scores = self.score(0, keys)
        key_at = lax.broadcasted_iota(jnp.int32, scores.shape, 0)
        query_at = lax.broadcasted_iota(jnp.int32, scores.shape, 1)
        scores = jnp.where(key_at <= query_at, scores, LOW)
        self.gather(0, values, self.settle(0, scores))
        @pl.loop(1, 4)
        def _(piece):
            @pl.when((self.place ^ piece) > self.place)
            def _():
                self.level(piece, keys, values)

    def finish(self, outs):
        for piece in range(4):
            columns = self.columns(piece)
            total = self.stat_ref[1:2, columns]
            some = total > 0.0
            safe = jnp.where(some, total, 1.0)
            outs[piece][0:HEAD, :] = (self.acc_ref[:, columns] / safe).astype(BF)
            level = jnp.where(some, self.stat_ref[0:1, columns] + jnp.log2(safe), LOW)
            high = level.astype(BF)
            rest = level - high.astype(F32)
            middle = rest.astype(BF)
            low = (rest - middle.astype(F32)).astype(BF)
            row = lax.broadcasted_iota(jnp.int32, (16, ROWS), 0)
            parts = jnp.where(
                row == 0,
                high.astype(F32),
                jnp.where(row == 1, middle.astype(F32), jnp.where(row == 2, low.astype(F32), 0.0)),
            )
            outs[piece][HEAD:PAY, :] = parts.astype(BF)


def attend_first(head, q0, q1, q2, q3, own, up, down, stat_ref, acc_ref, query_ref, chunk_ref):
    plane = lax.axis_index("z")
    flash = Flash(head, spot(), (q0, q1, q2, q3), stat_ref, acc_ref, query_ref)
    flash.start()
    flash.diagonal(*unpack(own[0:ROWS, :], own[ROWS : 2 * ROWS, :]))
    either(flash, plane, 1, up, down, chunk_ref)


def either(flash, plane, distance, up, down, chunk_ref):
    @pl.loop(0, 2)
    def _(side):
        for at, active, part in ((0, plane >= distance, up), (1, plane + distance >= 8, down)):

            @pl.when(active & (side == at))
            def _():
                chunk_ref[...] = part[...]

        @pl.when(jnp.where(side == 0, plane >= distance, plane + distance >= 8))
        def _():
            flash.full(*unpack(chunk_ref[0:ROWS, :], chunk_ref[ROWS : 2 * ROWS, :]))


def attend_next(head, distance, q0, q1, q2, q3, up, down, stat_in, acc_in, stat_ref, acc_ref, query_ref, chunk_ref):
    stat_ref[...] = stat_in[...]
    acc_ref[...] = acc_in[...]
    flash = Flash(head, spot(), (q0, q1, q2, q3), stat_ref, acc_ref, query_ref)
    either(flash, lax.axis_index("z"), distance, up, down, chunk_ref)


def attend_last(head, q0, q1, q2, q3, up, down, stat_in, acc_in, *others):
    o0, o1, o2, o3, stat_ref, acc_ref, query_ref = others[-7:]
    stat_ref[...] = stat_in[...]
    acc_ref[...] = acc_in[...]
    flash = Flash(head, spot(), (q0, q1, q2, q3), stat_ref, acc_ref, query_ref)

    @pl.when(lax.axis_index("z") >= 4)
    def _():
        flash.full(*unpack(up[...], down[...]))

    flash.finish((o0, o1, o2, o3))


def merge(p0, p1, p2, p3, *others):
    out_ref = others[-1]
    pieces = (p0, p1, p2, p3)
    levels = []
    for piece in pieces:
        parts = piece[HEAD:PAY, :].astype(F32)
        levels.append(parts[0:1, :] + parts[1:2, :] + parts[2:3, :])
    top = functools.reduce(jnp.maximum, levels)
    shares = [jnp.exp2(level - top) for level in levels]
    total = functools.reduce(jnp.add, shares)
    mixed = sum(
        piece[0:HEAD, :].astype(F32) * (share / total) for piece, share in zip(pieces, shares)
    )
    out_ref[...] = mixed.T.astype(BF)


def project(*refs):
    near, far, weight, out_ref = refs[:8], refs[8:16], refs[16], refs[17]
    total = None
    for at in range(8):
        left = jnp.concatenate([near[at][...], far[at][...]], axis=1)
        term = jnp.dot(left, weight[at], preferred_element_type=F32)
        total = term if total is None else total + term
    out_ref[...] = total.astype(out_ref.dtype)


def hold(values, *after):
    count = len(values)
    return pl.pallas_call(
        lambda *refs: None,
        out_shape=tuple(jax.ShapeDtypeStruct(v.shape, v.dtype) for v in values),
        in_specs=[HBM] * (count + len(after)),
        out_specs=(HBM,) * count,
        input_output_aliases={i: i for i in range(count)},
        compiler_params=SMALL,
    )(*values, *after)


def turn(value, axis, size, step):
    return lax.ppermute(value, axis, [(i, (i + step) % size) for i in range(size)])


def around(own):
    return [
        part
        for half in (own, turn(own, "xh", 2, 1))
        for part in (half, turn(half, "y", 4, -1), turn(half, "y", 4, 1), turn(half, "y", 4, 2))
    ]


def cut(w_far, _, mine, other, strip, sem):
    first = lax.axis_index("c") * HEAD
    copy = pltpu.make_async_copy(w_far.at[pl.ds(pl.multiple_of(first, HEAD), HEAD), :], strip, sem)
    copy.start()
    copy.wait()
    for out, side in ((mine, lax.axis_index("xh")), (other, lax.axis_index("xh") ^ 1)):
        out[...] = strip[:, pl.ds(pl.multiple_of(side * (4 * ROWS), 4 * ROWS), 4 * ROWS)]


def split(mine, other, _, *outs):
    for out, dy in zip(outs, (0, 1, 3, 2)):
        columns = pl.ds(pl.multiple_of(((lax.axis_index("y") + 4 - dy) & 3) * ROWS, ROWS), ROWS)
        out[0:HEAD, :] = mine[:, columns]
        out[HEAD : 2 * HEAD, :] = other[:, columns]


def pile(*refs):
    for at in range(4):
        refs[4][at * 2 * HEAD : (at + 1) * 2 * HEAD, :] = refs[at][...]


def both(mine, other, weight_ref):
    here = lax.axis_index("c")
    for at in range(8):
        piece = (at % 4) * 2 * HEAD + (at // 4) * HEAD
        for index, part in ((here, mine), (1 - here, other)):
            rows = pl.ds(pl.multiple_of(index * HEAD, HEAD), HEAD)
            weight_ref[at, rows, :] = part[piece : piece + HEAD, :]


def halve(up, down, first, second):
    first[...] = up[0:ROWS, :]
    second[...] = down[ROWS : 2 * ROWS, :]


def swap4(value, e):
    return lax.ppermute(value, ("xl", "c"), [(i, i ^ e) for i in range(4)])


def local(queries, keys, values, w_out):
    qt, kv0, kv1 = pl.pallas_call(
        prepare,
        out_shape=(
            jax.ShapeDtypeStruct((2 * HEAD, ROWS), BF),
            jax.ShapeDtypeStruct((2 * ROWS, HEAD), BF),
            jax.ShapeDtypeStruct((2 * ROWS, HEAD), BF),
        ),
        in_specs=[HBM] * 3,
        out_specs=(VMEM,) * 3,
        scratch_shapes=(*[pltpu.VMEM((ROWS, 2 * HEAD), BF)] * 3, pltpu.SemaphoreType.DMA((3,))),
        compiler_params=LARGE,
        cost_estimate=pl.CostEstimate(flops=0, bytes_accessed=3 * 2**19, transcendentals=0),
    )(queries, keys, values)
    state_shapes = (jax.ShapeDtypeStruct((8, 4 * ROWS), F32), jax.ShapeDtypeStruct((HEAD, 4 * ROWS), F32))
    state_scratch = (pltpu.VMEM((8, 4 * ROWS), F32), pltpu.VMEM((HEAD, 4 * ROWS), F32))
    pay_shapes = tuple(jax.ShapeDtypeStruct((PAY, ROWS), BF) for _ in range(4))
    query_scratch = (pltpu.VMEM((HEAD, 4 * ROWS), BF),)
    chunk_scratch = (*query_scratch, pltpu.VMEM((2 * ROWS, HEAD), BF))
    costs = dict(flops=4 * 2**30, bytes_accessed=4 * 2**21, exps=0)

    own = [kv0, kv1]
    ups, downs = [turn(kv0, "z", 8, 1)], [turn(kv0, "z", 8, -1)]
    q_cross, q_core = turn(qt, "xl", 2, 1), turn(qt, "c", 2, 1)
    (q_cross,) = hold((q_cross,), ups[0], downs[0])
    ups.append(turn(own[1], "z", 8, 1))
    downs.append(turn(own[1], "z", 8, -1))
    q_pieces = [qt, q_core, q_cross, turn(q_cross, "c", 2, 1)]

    mine, other = call(
        cut,
        (jax.ShapeDtypeStruct((HEAD, 4 * ROWS), BF),) * 2,
        (w_out, q_pieces[3]),
        scratch=(pltpu.VMEM((HEAD, 8 * ROWS), BF), pltpu.SemaphoreType.DMA),
        far=2,
    )
    other = turn(other, "xh", 2, 1)

    states = [
        call(
            functools.partial(attend_first, head),
            state_shapes,
            (*q_pieces, own[head], ups[head], downs[head]),
            scratch=chunk_scratch,
            **costs,
        )
        for head in range(2)
    ]
    strips = list(call(split, (jax.ShapeDtypeStruct((2 * HEAD, ROWS), BF),) * 4, (mine, other, states[0][0]), far=1))
    strips[1] = turn(strips[1], "y", 4, -1)
    for at, dy in ((2, -1), (3, 2)):
        (held,) = hold((strips[at],), strips[at - 1])
        strips[at] = turn(held, "y", 4, -dy)
    before = {(2, 1): (other,), (3, 1): strips[1:2]}
    for distance in (2, 3):
        for head in range(2):
            up, down = turn(ups[head], "z", 8, 1), turn(downs[head], "z", 8, -1)
            ups[head], downs[head] = hold((up, down), states[head][0], *before.get((distance, head), ()))
            states[head] = call(
                functools.partial(attend_next, head, distance),
                state_shapes,
                (*q_pieces, ups[head], downs[head], *states[head]),
                scratch=chunk_scratch,
                aliases={6: 0, 7: 1},
                **costs,
            )
    lasts = []
    for head in range(2):
        halves = call(halve, (jax.ShapeDtypeStruct((ROWS, HEAD), BF),) * 2, (ups[head], downs[head]))
        lasts.append((turn(halves[0], "z", 8, 1), turn(halves[1], "z", 8, -1)))
    mine = call(pile, jax.ShapeDtypeStruct((8 * HEAD, ROWS), BF), tuple(strips))
    terms = []
    for head in range(2):
        payload = call(
            functools.partial(attend_last, head),
            pay_shapes,
            (*q_pieces, *lasts[head], *states[head], strips[2 + head], lasts[1][1] if head == 0 else early[1]),
            scratch=(*state_scratch, *query_scratch),
            far=2,
            **costs,
        )
        if head == 1:
            payload = hold(payload, terms[0])
        early = [payload[0]] + [swap4(payload[e], e) for e in (1, 2, 3)]
        out = call(merge, jax.ShapeDtypeStruct((ROWS, HEAD), BF), (*early, *terms[1:5]), far=4 * head)
        terms += around(out)
    (mine,) = hold((mine,), terms[8])
    other = turn(mine, "c", 2, 1)
    weight = call(both, jax.ShapeDtypeStruct((8, 2 * HEAD, ROWS), BF), (mine, other))
    return call(
        project,
        jax.ShapeDtypeStruct((ROWS, ROWS), BF),
        (*terms, weight),
        flops=2**30,
        bytes_accessed=6 * 2**20,
    )


def solution(mesh):
    fine = Mesh(mesh.devices.reshape(8, 2, 2, 2, 4), ("z", "xl", "c", "xh", "y"))
    ctx, head = ("z", "xl", "c"), ("xh", "y")
    in_specs = (P(ctx, head), P(ctx, head), P(ctx, head), P(head, None))
    return jax.shard_map(
        local, mesh=fine, in_specs=in_specs, out_specs=P(ctx, head), check_vma=False
    )
```

```python
import functools

import jax
import jax.numpy as jnp
from jax import lax
from jax.experimental import pallas as pl
from jax.experimental.pallas import tpu as pltpu
from jax.sharding import Mesh, PartitionSpec as P

HEAD = 128
ROWS = 512
HALF = 256
REACH = 100.0
PAY = HEAD + 16
LOG2E = 1.4426950408889634
SCALE = HEAD ** (-0.5) * LOG2E
LOW = -1e30
BF = jnp.bfloat16
F32 = jnp.float32
VMEM = pl.BlockSpec(memory_space=pltpu.VMEM)
HBM = pl.BlockSpec(memory_space=pl.ANY)
ARGUMENT = pl.BlockSpec(memory_space=pltpu.HBM)
SMEM = pl.BlockSpec(memory_space=pltpu.SMEM)
PARAMS = pltpu.CompilerParams(vmem_limit_bytes=24 * 1024 * 1024)
LARGE = pltpu.CompilerParams(vmem_limit_bytes=8 * 1024 * 1024)
SMALL = pltpu.CompilerParams(vmem_limit_bytes=8 * 1024 * 1024)


def call(kernel, shapes, operands, scratch=(), flops=0, bytes_accessed=0, exps=0, smem=0, far=0, aliases=None):
    return pl.pallas_call(
        kernel,
        out_shape=shapes,
        in_specs=[SMEM] * smem + [VMEM] * (len(operands) - smem - far) + [HBM] * far,
        out_specs=jax.tree.map(lambda _: VMEM, shapes),
        scratch_shapes=scratch,
        input_output_aliases=aliases or {},
        compiler_params=PARAMS,
        cost_estimate=pl.CostEstimate(flops=flops, bytes_accessed=bytes_accessed, transcendentals=exps),
    )(*operands)


def prepare(q_far, k_far, v_far, qt_ref, kv0_ref, kv1_ref, q_ref, k_ref, v_ref, sem):
    copies = [
        pltpu.make_async_copy(far, near, sem.at[at])
        for at, (far, near) in enumerate(((q_far, q_ref), (k_far, k_ref), (v_far, v_ref)))
    ]
    for copy in copies:
        copy.start()
    for copy in copies:
        copy.wait()
    turned = q_ref[...].T
    qt_ref[...] = turned
    for head, out in ((0, kv0_ref), (1, kv1_ref)):
        columns = slice(head * HEAD, (head + 1) * HEAD)
        for half in range(2):
            at = half * ROWS
            out[at : at + HALF, :] = k_ref[half * HALF : (half + 1) * HALF, columns]
            for block in range(2):
                rows = slice(half * HALF + block * HEAD, half * HALF + (block + 1) * HEAD)
                to = at + HALF + block * HEAD
                out[to : to + HEAD, :] = v_ref[rows, columns].T


def unpack(first, second):
    keys = jnp.concatenate([first[0:HALF, :], second[0:HALF, :]], axis=0)
    blocks = [part[HALF + b * HEAD : HALF + (b + 1) * HEAD, :] for part in (first, second) for b in (0, 1)]
    return keys, jnp.concatenate(blocks, axis=1)


def spot():
    return lax.axis_index("xl") * 2 + lax.axis_index("c")


class Flash:
    def __init__(self, head, place, queries, stat_ref, acc_ref, query_ref):
        self.place, self.query_ref = place, query_ref
        for piece, query in enumerate(queries):
            query_ref[:, self.columns(piece)] = query[head * HEAD : (head + 1) * HEAD, :]
        self.stat_ref, self.acc_ref = stat_ref, acc_ref

    def columns(self, piece):
        if isinstance(piece, int):
            return slice(piece * ROWS, (piece + 1) * ROWS)
        return pl.ds(pl.multiple_of(piece * ROWS, ROWS), ROWS)

    def query(self, piece):
        return self.query_ref[:, self.columns(piece)]

    def start(self):
        width = 4 * ROWS
        self.stat_ref[0:1, :] = jnp.full((1, width), LOW, F32)
        self.stat_ref[1:2, :] = jnp.zeros((1, width), F32)
        self.acc_ref[...] = jnp.zeros(self.acc_ref.shape, F32)
        query = self.query_ref[...].astype(F32)
        self.stat_ref[2:3, :] = jnp.sqrt(jnp.sum(query * query, axis=0, keepdims=True)) * SCALE

    def score(self, piece, keys):
        return jnp.dot(keys, self.query(piece), preferred_element_type=F32) * SCALE

    def settle(self, piece, scores):
        columns = self.columns(piece)
        old = self.stat_ref[0:1, columns]
        new = jnp.maximum(old, jnp.max(scores, axis=0, keepdims=True))
        weights = jnp.exp2(scores - new)
        fade = jnp.exp2(old - new)
        self.stat_ref[0:1, columns] = new
        self.stat_ref[1:2, columns] = self.stat_ref[1:2, columns] * fade + jnp.sum(
            weights, axis=0, keepdims=True
        )
        self.acc_ref[:, columns] = self.acc_ref[:, columns] * fade
        return weights.astype(BF)

    def keep(self, piece, scores):
        columns = self.columns(piece)
        weights = jnp.exp2(scores - self.stat_ref[0:1, columns])
        self.stat_ref[1:2, columns] = self.stat_ref[1:2, columns] + jnp.sum(
            weights, axis=0, keepdims=True
        )
        return weights.astype(BF)

    def gather(self, piece, values, weights):
        columns = self.columns(piece)
        self.acc_ref[:, columns] = self.acc_ref[:, columns] + jnp.dot(
            values, weights, preferred_element_type=F32
        )

    def absorb(self, keys, values):
        following, waiting = self.score(0, keys), None
        for piece in range(4):
            scores = following
            if piece < 3:
                following = self.score(piece + 1, keys)
            if waiting is not None:
                self.gather(*waiting)
            waiting = (piece, values, self.keep(piece, scores))
        self.gather(*waiting)

    def level(self, piece, keys, values):
        self.gather(piece, values, self.settle(piece, self.score(piece, keys)))

    def full(self, keys, values):
        sizes = keys.astype(F32)
        longest = jnp.max(jnp.sum(sizes * sizes, axis=1, keepdims=True))
        reach = jnp.max(self.stat_ref[2:3, :]) ** 2 * longest
        lowest = jnp.min(self.stat_ref[0:1, :])
        room = lowest + REACH
        stays = (room > 0.0) & (reach <= room * room)

        @pl.when(stays)
        def _():
            self.absorb(keys, values)

        @pl.when(jnp.logical_not(stays))
        def _():
            @pl.loop(0, 4)
            def _(piece):
                self.level(piece, keys, values)

    def diagonal(self, keys, values):
        scores = self.score(0, keys)
        key_at = lax.broadcasted_iota(jnp.int32, scores.shape, 0)
        query_at = lax.broadcasted_iota(jnp.int32, scores.shape, 1)
        scores = jnp.where(key_at <= query_at, scores, LOW)
        self.gather(0, values, self.settle(0, scores))
        @pl.loop(1, 4)
        def _(piece):
            @pl.when((self.place ^ piece) > self.place)
            def _():
                self.level(piece, keys, values)

    def finish(self, outs):
        for piece in range(4):
            columns = self.columns(piece)
            total = self.stat_ref[1:2, columns]
            some = total > 0.0
            safe = jnp.where(some, total, 1.0)
            outs[piece][0:HEAD, :] = (self.acc_ref[:, columns] / safe).astype(BF)
            level = jnp.where(some, self.stat_ref[0:1, columns] + jnp.log2(safe), LOW)
            high = level.astype(BF)
            rest = level - high.astype(F32)
            middle = rest.astype(BF)
            low = (rest - middle.astype(F32)).astype(BF)
            row = lax.broadcasted_iota(jnp.int32, (16, ROWS), 0)
            parts = jnp.where(
                row == 0,
                high.astype(F32),
                jnp.where(row == 1, middle.astype(F32), jnp.where(row == 2, low.astype(F32), 0.0)),
            )
            outs[piece][HEAD:PAY, :] = parts.astype(BF)


def attend_first(head, q0, q1, q2, q3, own, up, down, stat_ref, acc_ref, query_ref, chunk_ref):
    plane = lax.axis_index("z")
    flash = Flash(head, spot(), (q0, q1, q2, q3), stat_ref, acc_ref, query_ref)
    flash.start()
    flash.diagonal(*unpack(own[0:ROWS, :], own[ROWS : 2 * ROWS, :]))
    either(flash, plane, 1, up, down, chunk_ref)


def either(flash, plane, distance, up, down, chunk_ref):
    @pl.loop(0, 2)
    def _(side):
        for at, active, part in ((0, plane >= distance, up), (1, plane + distance >= 8, down)):

            @pl.when(active & (side == at))
            def _():
                chunk_ref[...] = part[...]

        @pl.when(jnp.where(side == 0, plane >= distance, plane + distance >= 8))
        def _():
            flash.full(*unpack(chunk_ref[0:ROWS, :], chunk_ref[ROWS : 2 * ROWS, :]))


def attend_next(head, distance, q0, q1, q2, q3, up, down, stat_in, acc_in, stat_ref, acc_ref, query_ref, chunk_ref):
    stat_ref[...] = stat_in[...]
    acc_ref[...] = acc_in[...]
    flash = Flash(head, spot(), (q0, q1, q2, q3), stat_ref, acc_ref, query_ref)
    either(flash, lax.axis_index("z"), distance, up, down, chunk_ref)


def attend_last(head, q0, q1, q2, q3, up, down, stat_in, acc_in, *others):
    o0, o1, o2, o3, stat_ref, acc_ref, query_ref = others[-7:]
    stat_ref[...] = stat_in[...]
    acc_ref[...] = acc_in[...]
    flash = Flash(head, spot(), (q0, q1, q2, q3), stat_ref, acc_ref, query_ref)

    @pl.when(lax.axis_index("z") >= 4)
    def _():
        flash.full(*unpack(up[...], down[...]))

    flash.finish((o0, o1, o2, o3))


def merge(p0, p1, p2, p3, *others):
    out_ref = others[-1]
    pieces = (p0, p1, p2, p3)
    levels = []
    for piece in pieces:
        parts = piece[HEAD:PAY, :].astype(F32)
        levels.append(parts[0:1, :] + parts[1:2, :] + parts[2:3, :])
    top = functools.reduce(jnp.maximum, levels)
    shares = [jnp.exp2(level - top) for level in levels]
    total = functools.reduce(jnp.add, shares)
    mixed = sum(
        piece[0:HEAD, :].astype(F32) * (share / total) for piece, share in zip(pieces, shares)
    )
    out_ref[...] = mixed.T.astype(BF)


def project(head, *refs):
    parts, weight, out_ref = refs[:8], refs[8], refs[-1]
    total = refs[9][...] if len(refs) > 10 else None
    for at in range(0, 8, 2):
        left = jnp.concatenate([parts[at][...], parts[at + 1][...]], axis=1)
        rows = slice(head * HEAD, (head + 1) * HEAD)
        right = jnp.concatenate([weight[at, rows, :], weight[at + 1, rows, :]], axis=0)
        term = jnp.dot(left, right, preferred_element_type=F32)
        total = term if total is None else total + term
    out_ref[...] = total.astype(out_ref.dtype)


def hold(values, *after):
    count = len(values)
    return pl.pallas_call(
        lambda *refs: None,
        out_shape=tuple(jax.ShapeDtypeStruct(v.shape, v.dtype) for v in values),
        in_specs=[HBM] * (count + len(after)),
        out_specs=(HBM,) * count,
        input_output_aliases={i: i for i in range(count)},
        compiler_params=SMALL,
    )(*values, *after)


def turn(value, axis, size, step):
    return lax.ppermute(value, axis, [(i, (i + step) % size) for i in range(size)])


def around(own):
    return [
        part
        for half in (own, turn(own, "xh", 2, 1))
        for part in (half, turn(half, "y", 4, -1), turn(half, "y", 4, 1), turn(half, "y", 4, 2))
    ]


def cut(w_far, _, mine, other, strip, sem):
    first = lax.axis_index("c") * HEAD
    copy = pltpu.make_async_copy(w_far.at[pl.ds(pl.multiple_of(first, HEAD), HEAD), :], strip, sem)
    copy.start()
    copy.wait()
    for out, side in ((mine, lax.axis_index("xh")), (other, lax.axis_index("xh") ^ 1)):
        out[...] = strip[:, pl.ds(pl.multiple_of(side * (4 * ROWS), 4 * ROWS), 4 * ROWS)]


def split(mine, other, _, *outs):
    for out, dy in zip(outs, (0, 1, 3, 2)):
        columns = pl.ds(pl.multiple_of(((lax.axis_index("y") + 4 - dy) & 3) * ROWS, ROWS), ROWS)
        out[0:HEAD, :] = mine[:, columns]
        out[HEAD : 2 * HEAD, :] = other[:, columns]


def pile(*refs):
    for at in range(4):
        refs[4][at * 2 * HEAD : (at + 1) * 2 * HEAD, :] = refs[at][...]


def both(mine, other, weight_ref):
    here = lax.axis_index("c")
    for at in range(8):
        piece = (at % 4) * 2 * HEAD + (at // 4) * HEAD
        for index, part in ((here, mine), (1 - here, other)):
            rows = pl.ds(pl.multiple_of(index * HEAD, HEAD), HEAD)
            weight_ref[at, rows, :] = part[piece : piece + HEAD, :]


def halve(up, down, first, second):
    first[...] = up[0:ROWS, :]
    second[...] = down[ROWS : 2 * ROWS, :]


def swap4(value, e):
    return lax.ppermute(value, ("xl", "c"), [(i, i ^ e) for i in range(4)])


def local(queries, keys, values, w_out):
    qt, kv0, kv1 = pl.pallas_call(
        prepare,
        out_shape=(
            jax.ShapeDtypeStruct((2 * HEAD, ROWS), BF),
            jax.ShapeDtypeStruct((2 * ROWS, HEAD), BF),
            jax.ShapeDtypeStruct((2 * ROWS, HEAD), BF),
        ),
        in_specs=[ARGUMENT] * 3,
        out_specs=(VMEM,) * 3,
        scratch_shapes=(*[pltpu.VMEM((ROWS, 2 * HEAD), BF)] * 3, pltpu.SemaphoreType.DMA((3,))),
        compiler_params=LARGE,
        cost_estimate=pl.CostEstimate(flops=0, bytes_accessed=3 * 2**19, transcendentals=0),
    )(queries, keys, values)
    state_shapes = (jax.ShapeDtypeStruct((8, 4 * ROWS), F32), jax.ShapeDtypeStruct((HEAD, 4 * ROWS), F32))
    state_scratch = (pltpu.VMEM((8, 4 * ROWS), F32), pltpu.VMEM((HEAD, 4 * ROWS), F32))
    pay_shapes = tuple(jax.ShapeDtypeStruct((PAY, ROWS), BF) for _ in range(4))
    query_scratch = (pltpu.VMEM((HEAD, 4 * ROWS), BF),)
    chunk_scratch = (*query_scratch, pltpu.VMEM((2 * ROWS, HEAD), BF))
    costs = dict(flops=4 * 2**30, bytes_accessed=4 * 2**21, exps=0)

    own = [kv0, kv1]
    ups, downs = [turn(kv0, "z", 8, 1)], [turn(kv0, "z", 8, -1)]
    q_cross, q_core = turn(qt, "xl", 2, 1), turn(qt, "c", 2, 1)
    (q_cross,) = hold((q_cross,), ups[0], downs[0])
    ups.append(turn(own[1], "z", 8, 1))
    downs.append(turn(own[1], "z", 8, -1))
    q_pieces = [qt, q_core, q_cross, turn(q_cross, "c", 2, 1)]

    mine, other = pl.pallas_call(
        cut,
        out_shape=(jax.ShapeDtypeStruct((HEAD, 4 * ROWS), BF),) * 2,
        in_specs=[ARGUMENT, HBM],
        out_specs=(VMEM,) * 2,
        scratch_shapes=(pltpu.VMEM((HEAD, 8 * ROWS), BF), pltpu.SemaphoreType.DMA),
        compiler_params=SMALL,
    )(w_out, q_pieces[3])
    other = turn(other, "xh", 2, 1)

    states = [
        call(
            functools.partial(attend_first, head),
            state_shapes,
            (*q_pieces, own[head], ups[head], downs[head]),
            scratch=chunk_scratch,
            **costs,
        )
        for head in range(2)
    ]
    strips = list(call(split, (jax.ShapeDtypeStruct((2 * HEAD, ROWS), BF),) * 4, (mine, other, states[0][0]), far=1))
    strips[1] = turn(strips[1], "y", 4, -1)
    for at, dy in ((2, -1), (3, 2)):
        (held,) = hold((strips[at],), strips[at - 1])
        strips[at] = turn(held, "y", 4, -dy)
    before = {(2, 1): (other,), (3, 1): strips[1:2]}
    for distance in (2, 3):
        for head in range(2):
            up, down = turn(ups[head], "z", 8, 1), turn(downs[head], "z", 8, -1)
            ups[head], downs[head] = hold((up, down), states[head][0], *before.get((distance, head), ()))
            states[head] = call(
                functools.partial(attend_next, head, distance),
                state_shapes,
                (*q_pieces, ups[head], downs[head], *states[head]),
                scratch=chunk_scratch,
                aliases={6: 0, 7: 1},
                **costs,
            )
    lasts = []
    for head in range(2):
        halves = call(halve, (jax.ShapeDtypeStruct((ROWS, HEAD), BF),) * 2, (ups[head], downs[head]))
        lasts.append((turn(halves[0], "z", 8, 1), turn(halves[1], "z", 8, -1)))
    mine = call(pile, jax.ShapeDtypeStruct((8 * HEAD, ROWS), BF), tuple(strips))
    terms = []
    for head in range(2):
        payload = call(
            functools.partial(attend_last, head),
            pay_shapes,
            (*q_pieces, *lasts[head], *states[head], *(lasts[1] if head == 0 else (strips[3], early[1]))),
            scratch=(*state_scratch, *query_scratch),
            far=2,
            **costs,
        )
        if head == 1:
            payload = hold(payload, terms[4])
        early = [payload[0]] + [swap4(payload[e], e) for e in (1, 2, 3)]
        out = call(merge, jax.ShapeDtypeStruct((ROWS, HEAD), BF), (*early, *[terms[at] for at in (1,2,3,5,6) if head == 1]), far=5 * head)
        terms += around(out)
    (mine,) = hold((mine,), terms[8])
    other = turn(mine, "c", 2, 1)
    weight = call(both, jax.ShapeDtypeStruct((8, 2 * HEAD, ROWS), BF), (mine, other))
    total = call(functools.partial(project, 0), jax.ShapeDtypeStruct((ROWS, ROWS), F32), (*terms[:8], weight))
    return call(functools.partial(project, 1), jax.ShapeDtypeStruct((ROWS, ROWS), BF), (*terms[8:], weight, total))


def solution(mesh):
    fine = Mesh(mesh.devices.reshape(8, 2, 2, 2, 4), ("z", "xl", "c", "xh", "y"))
    ctx, head = ("z", "xl", "c"), ("xh", "y")
    in_specs = (P(ctx, head), P(ctx, head), P(ctx, head), P(head, None))
    return jax.shard_map(
        local, mesh=fine, in_specs=in_specs, out_specs=P(ctx, head), check_vma=False
    )
```

```python
import functools

import jax
import jax.numpy as jnp
from jax import lax
from jax.experimental import pallas as pl
from jax.experimental.pallas import tpu as pltpu
from jax.sharding import Mesh, PartitionSpec as P

HEAD = 128
ROWS = 512
HALF = 256
REACH = 100.0
PAY = HEAD + 16
LOG2E = 1.4426950408889634
SCALE = HEAD ** (-0.5) * LOG2E
LOW = -1e30
BF = jnp.bfloat16
F32 = jnp.float32
VMEM = pl.BlockSpec(memory_space=pltpu.VMEM)
HBM = pl.BlockSpec(memory_space=pl.ANY)
ARGUMENT = pl.BlockSpec(memory_space=pltpu.HBM)
SMEM = pl.BlockSpec(memory_space=pltpu.SMEM)
PARAMS = pltpu.CompilerParams(vmem_limit_bytes=24 * 1024 * 1024)
LARGE = pltpu.CompilerParams(vmem_limit_bytes=8 * 1024 * 1024)
SMALL = pltpu.CompilerParams(vmem_limit_bytes=8 * 1024 * 1024)


def call(kernel, shapes, operands, scratch=(), flops=0, bytes_accessed=0, exps=0, smem=0, far=0, aliases=None):
    return pl.pallas_call(
        kernel,
        out_shape=shapes,
        in_specs=[SMEM] * smem + [VMEM] * (len(operands) - smem - far) + [HBM] * far,
        out_specs=jax.tree.map(lambda _: VMEM, shapes),
        scratch_shapes=scratch,
        input_output_aliases=aliases or {},
        compiler_params=PARAMS,
        cost_estimate=pl.CostEstimate(flops=flops, bytes_accessed=bytes_accessed, transcendentals=exps),
    )(*operands)


def prepare(q_far, k_far, v_far, qt_ref, kv0_ref, kv1_ref, q_ref, k_ref, v_ref, sem):
    copies = [
        pltpu.make_async_copy(far, near, sem.at[at])
        for at, (far, near) in enumerate(((q_far, q_ref), (k_far, k_ref), (v_far, v_ref)))
    ]
    for copy in copies:
        copy.start()
    for copy in copies:
        copy.wait()
    turned = q_ref[...].T
    qt_ref[...] = turned
    for head, out in ((0, kv0_ref), (1, kv1_ref)):
        columns = slice(head * HEAD, (head + 1) * HEAD)
        for half in range(2):
            at = half * ROWS
            out[at : at + HALF, :] = k_ref[half * HALF : (half + 1) * HALF, columns]
            for block in range(2):
                rows = slice(half * HALF + block * HEAD, half * HALF + (block + 1) * HEAD)
                to = at + HALF + block * HEAD
                out[to : to + HEAD, :] = v_ref[rows, columns].T


def unpack(first, second):
    keys = jnp.concatenate([first[0:HALF, :], second[0:HALF, :]], axis=0)
    blocks = [part[HALF + b * HEAD : HALF + (b + 1) * HEAD, :] for part in (first, second) for b in (0, 1)]
    return keys, jnp.concatenate(blocks, axis=1)


def spot():
    return lax.axis_index("xl") * 2 + lax.axis_index("c")


class Flash:
    def __init__(self, head, place, queries, stat_ref, acc_ref, query_ref):
        self.place, self.query_ref = place, query_ref
        for piece, query in enumerate(queries):
            query_ref[:, self.columns(piece)] = query[head * HEAD : (head + 1) * HEAD, :]
        self.stat_ref, self.acc_ref = stat_ref, acc_ref

    def columns(self, piece):
        if isinstance(piece, int):
            return slice(piece * ROWS, (piece + 1) * ROWS)
        return pl.ds(pl.multiple_of(piece * ROWS, ROWS), ROWS)

    def query(self, piece):
        return self.query_ref[:, self.columns(piece)]

    def start(self):
        width = 4 * ROWS
        self.stat_ref[0:1, :] = jnp.full((1, width), LOW, F32)
        self.stat_ref[1:2, :] = jnp.zeros((1, width), F32)
        self.acc_ref[...] = jnp.zeros(self.acc_ref.shape, F32)
        query = self.query_ref[...].astype(F32)
        self.stat_ref[2:3, :] = jnp.sqrt(jnp.sum(query * query, axis=0, keepdims=True)) * SCALE

    def score(self, piece, keys):
        return jnp.dot(keys, self.query(piece), preferred_element_type=F32) * SCALE

    def settle(self, piece, scores):
        columns = self.columns(piece)
        old = self.stat_ref[0:1, columns]
        new = jnp.maximum(old, jnp.max(scores, axis=0, keepdims=True))
        weights = jnp.exp2(scores - new)
        fade = jnp.exp2(old - new)
        self.stat_ref[0:1, columns] = new
        self.stat_ref[1:2, columns] = self.stat_ref[1:2, columns] * fade + jnp.sum(
            weights, axis=0, keepdims=True
        )
        self.acc_ref[:, columns] = self.acc_ref[:, columns] * fade
        return weights.astype(BF)

    def keep(self, piece, scores):
        columns = self.columns(piece)
        weights = jnp.exp2(scores - self.stat_ref[0:1, columns])
        self.stat_ref[1:2, columns] = self.stat_ref[1:2, columns] + jnp.sum(
            weights, axis=0, keepdims=True
        )
        return weights.astype(BF)

    def gather(self, piece, values, weights):
        columns = self.columns(piece)
        self.acc_ref[:, columns] = self.acc_ref[:, columns] + jnp.dot(
            values, weights, preferred_element_type=F32
        )

    def absorb(self, keys, values):
        following, waiting = self.score(0, keys), None
        for piece in range(4):
            scores = following
            if piece < 3:
                following = self.score(piece + 1, keys)
            if waiting is not None:
                self.gather(*waiting)
            waiting = (piece, values, self.keep(piece, scores))
        self.gather(*waiting)

    def level(self, piece, keys, values):
        self.gather(piece, values, self.settle(piece, self.score(piece, keys)))

    def full(self, keys, values):
        sizes = keys.astype(F32)
        longest = jnp.max(jnp.sum(sizes * sizes, axis=1, keepdims=True))
        reach = jnp.max(self.stat_ref[2:3, :]) ** 2 * longest
        lowest = jnp.min(self.stat_ref[0:1, :])
        room = lowest + REACH
        stays = (room > 0.0) & (reach <= room * room)

        @pl.when(stays)
        def _():
            self.absorb(keys, values)

        @pl.when(jnp.logical_not(stays))
        def _():
            @pl.loop(0, 4)
            def _(piece):
                self.level(piece, keys, values)

    def diagonal(self, keys, values):
        scores = self.score(0, keys)
        key_at = lax.broadcasted_iota(jnp.int32, scores.shape, 0)
        query_at = lax.broadcasted_iota(jnp.int32, scores.shape, 1)
        scores = jnp.where(key_at <= query_at, scores, LOW)
        self.gather(0, values, self.settle(0, scores))
        @pl.loop(1, 4)
        def _(piece):
            @pl.when((self.place ^ piece) > self.place)
            def _():
                self.level(piece, keys, values)

    def finish(self, outs):
        for piece in range(4):
            columns = self.columns(piece)
            total = self.stat_ref[1:2, columns]
            some = total > 0.0
            safe = jnp.where(some, total, 1.0)
            outs[piece][0:HEAD, :] = (self.acc_ref[:, columns] / safe).astype(BF)
            level = jnp.where(some, self.stat_ref[0:1, columns] + jnp.log2(safe), LOW)
            high = level.astype(BF)
            rest = level - high.astype(F32)
            middle = rest.astype(BF)
            low = (rest - middle.astype(F32)).astype(BF)
            row = lax.broadcasted_iota(jnp.int32, (16, ROWS), 0)
            parts = jnp.where(
                row == 0,
                high.astype(F32),
                jnp.where(row == 1, middle.astype(F32), jnp.where(row == 2, low.astype(F32), 0.0)),
            )
            outs[piece][HEAD:PAY, :] = parts.astype(BF)


def attend_first(head, q0, q1, q2, q3, own, up, down, stat_ref, acc_ref, query_ref, chunk_ref):
    plane = lax.axis_index("z")
    flash = Flash(head, spot(), (q0, q1, q2, q3), stat_ref, acc_ref, query_ref)
    flash.start()
    flash.diagonal(*unpack(own[0:ROWS, :], own[ROWS : 2 * ROWS, :]))
    either(flash, plane, 1, up, down, chunk_ref)


def either(flash, plane, distance, up, down, chunk_ref):
    @pl.loop(0, 2)
    def _(side):
        for at, active, part in ((0, plane >= distance, up), (1, plane + distance >= 8, down)):

            @pl.when(active & (side == at))
            def _():
                chunk_ref[...] = part[...]

        @pl.when(jnp.where(side == 0, plane >= distance, plane + distance >= 8))
        def _():
            flash.full(*unpack(chunk_ref[0:ROWS, :], chunk_ref[ROWS : 2 * ROWS, :]))


def attend_next(head, distance, q0, q1, q2, q3, up, down, stat_in, acc_in, stat_ref, acc_ref, query_ref, chunk_ref):
    stat_ref[...] = stat_in[...]
    acc_ref[...] = acc_in[...]
    flash = Flash(head, spot(), (q0, q1, q2, q3), stat_ref, acc_ref, query_ref)
    either(flash, lax.axis_index("z"), distance, up, down, chunk_ref)


def attend_last(head, q0, q1, q2, q3, up, down, stat_in, acc_in, *others):
    o0, o1, o2, o3, stat_ref, acc_ref, query_ref = others[-7:]
    stat_ref[...] = stat_in[...]
    acc_ref[...] = acc_in[...]
    flash = Flash(head, spot(), (q0, q1, q2, q3), stat_ref, acc_ref, query_ref)

    @pl.when(lax.axis_index("z") >= 4)
    def _():
        flash.full(*unpack(up[...], down[...]))

    flash.finish((o0, o1, o2, o3))


def merge(p0, p1, p2, p3, *others):
    out_ref = others[-1]
    pieces = (p0, p1, p2, p3)
    levels = []
    for piece in pieces:
        parts = piece[HEAD:PAY, :].astype(F32)
        levels.append(parts[0:1, :] + parts[1:2, :] + parts[2:3, :])
    top = functools.reduce(jnp.maximum, levels)
    shares = [jnp.exp2(level - top) for level in levels]
    total = functools.reduce(jnp.add, shares)
    mixed = sum(
        piece[0:HEAD, :].astype(F32) * (share / total) for piece, share in zip(pieces, shares)
    )
    out_ref[...] = mixed.T.astype(BF)


def project(head, *refs):
    parts, weight, out_ref = refs[:8], refs[8], refs[-1]
    total = refs[9][...] if len(refs) > 10 else None
    for at in range(0, 8, 2):
        left = jnp.concatenate([parts[at][...], parts[at + 1][...]], axis=1)
        rows = slice(head * HEAD, (head + 1) * HEAD)
        right = jnp.concatenate([weight[at, rows, :], weight[at + 1, rows, :]], axis=0)
        term = jnp.dot(left, right, preferred_element_type=F32)
        total = term if total is None else total + term
    out_ref[...] = total.astype(out_ref.dtype)


def hold(values, *after):
    count = len(values)
    return pl.pallas_call(
        lambda *refs: None,
        out_shape=tuple(jax.ShapeDtypeStruct(v.shape, v.dtype) for v in values),
        in_specs=[HBM] * (count + len(after)),
        out_specs=(HBM,) * count,
        input_output_aliases={i: i for i in range(count)},
        compiler_params=SMALL,
    )(*values, *after)


def turn(value, axis, size, step):
    return lax.ppermute(value, axis, [(i, (i + step) % size) for i in range(size)])


def around(own):
    return [
        part
        for half in (own, turn(own, "xh", 2, 1))
        for part in (half, turn(half, "y", 4, -1), turn(half, "y", 4, 1), turn(half, "y", 4, 2))
    ]


def cut(w_far, _, mine, other, strip, sem):
    first = lax.axis_index("c") * HEAD
    copy = pltpu.make_async_copy(w_far.at[pl.ds(pl.multiple_of(first, HEAD), HEAD), :], strip, sem)
    copy.start()
    copy.wait()
    for out, side in ((mine, lax.axis_index("xh")), (other, lax.axis_index("xh") ^ 1)):
        out[...] = strip[:, pl.ds(pl.multiple_of(side * (4 * ROWS), 4 * ROWS), 4 * ROWS)]


def split(mine, other, _, *outs):
    for out, dy in zip(outs, (0, 1, 3, 2)):
        columns = pl.ds(pl.multiple_of(((lax.axis_index("y") + 4 - dy) & 3) * ROWS, ROWS), ROWS)
        out[0:HEAD, :] = mine[:, columns]
        out[HEAD : 2 * HEAD, :] = other[:, columns]


def pile(*refs):
    for at in range(4):
        refs[4][at * 2 * HEAD : (at + 1) * 2 * HEAD, :] = refs[at][...]


def both(mine, other, weight_ref):
    here = lax.axis_index("c")
    for at in range(8):
        piece = (at % 4) * 2 * HEAD + (at // 4) * HEAD
        for index, part in ((here, mine), (1 - here, other)):
            rows = pl.ds(pl.multiple_of(index * HEAD, HEAD), HEAD)
            weight_ref[at, rows, :] = part[piece : piece + HEAD, :]


def halve(up, down, first, second):
    first[...] = up[0:ROWS, :]
    second[...] = down[ROWS : 2 * ROWS, :]


def swap4(value, e):
    return lax.ppermute(value, ("xl", "c"), [(i, i ^ e) for i in range(4)])


def local(queries, keys, values, w_out):
    qt, kv0, kv1 = pl.pallas_call(
        prepare,
        out_shape=(
            jax.ShapeDtypeStruct((2 * HEAD, ROWS), BF),
            jax.ShapeDtypeStruct((2 * ROWS, HEAD), BF),
            jax.ShapeDtypeStruct((2 * ROWS, HEAD), BF),
        ),
        in_specs=[ARGUMENT] * 3,
        out_specs=(VMEM,) * 3,
        scratch_shapes=(*[pltpu.VMEM((ROWS, 2 * HEAD), BF)] * 3, pltpu.SemaphoreType.DMA((3,))),
        compiler_params=LARGE,
        cost_estimate=pl.CostEstimate(flops=2**36, bytes_accessed=0, transcendentals=0),
    )(queries, keys, values)
    state_shapes = (jax.ShapeDtypeStruct((8, 4 * ROWS), F32), jax.ShapeDtypeStruct((HEAD, 4 * ROWS), F32))
    state_scratch = (pltpu.VMEM((8, 4 * ROWS), F32), pltpu.VMEM((HEAD, 4 * ROWS), F32))
    pay_shapes = tuple(jax.ShapeDtypeStruct((PAY, ROWS), BF) for _ in range(4))
    query_scratch = (pltpu.VMEM((HEAD, 4 * ROWS), BF),)
    chunk_scratch = (*query_scratch, pltpu.VMEM((2 * ROWS, HEAD), BF))
    costs = dict(flops=4 * 2**30, bytes_accessed=4 * 2**21, exps=0)

    own = [kv0, kv1]
    ups, downs = [turn(kv0, "z", 8, 1)], [turn(kv0, "z", 8, -1)]
    q_cross, q_core = turn(qt, "xl", 2, 1), turn(qt, "c", 2, 1)
    (q_cross,) = hold((q_cross,), ups[0], downs[0])
    ups.append(turn(own[1], "z", 8, 1))
    downs.append(turn(own[1], "z", 8, -1))
    q_pieces = [qt, q_core, q_cross, turn(q_cross, "c", 2, 1)]

    mine, other = pl.pallas_call(
        cut,
        out_shape=(jax.ShapeDtypeStruct((HEAD, 4 * ROWS), BF),) * 2,
        in_specs=[ARGUMENT, HBM],
        out_specs=(VMEM,) * 2,
        scratch_shapes=(pltpu.VMEM((HEAD, 8 * ROWS), BF), pltpu.SemaphoreType.DMA),
        compiler_params=SMALL,
    )(w_out, q_pieces[3])
    other = turn(other, "xh", 2, 1)

    states = [
        call(
            functools.partial(attend_first, head),
            state_shapes,
            (*q_pieces, own[head], ups[head], downs[head]),
            scratch=chunk_scratch,
            **costs,
        )
        for head in range(2)
    ]
    strips = list(call(split, (jax.ShapeDtypeStruct((2 * HEAD, ROWS), BF),) * 4, (mine, other, states[0][0]), far=1))
    strips[1] = turn(strips[1], "y", 4, -1)
    for at, dy in ((2, -1), (3, 2)):
        (held,) = hold((strips[at],), strips[at - 1])
        strips[at] = turn(held, "y", 4, -dy)
    before = {(2, 1): (other,), (3, 1): strips[1:2]}
    for distance in (2, 3):
        for head in range(2):
            up, down = turn(ups[head], "z", 8, 1), turn(downs[head], "z", 8, -1)
            ups[head], downs[head] = hold((up, down), states[head][0], *before.get((distance, head), ()))
            states[head] = call(
                functools.partial(attend_next, head, distance),
                state_shapes,
                (*q_pieces, ups[head], downs[head], *states[head]),
                scratch=chunk_scratch,
                aliases={6: 0, 7: 1},
                **costs,
            )
    lasts = []
    for head in range(2):
        halves = call(halve, (jax.ShapeDtypeStruct((ROWS, HEAD), BF),) * 2, (ups[head], downs[head]))
        lasts.append((turn(halves[0], "z", 8, 1), turn(halves[1], "z", 8, -1)))
    mine = call(pile, jax.ShapeDtypeStruct((8 * HEAD, ROWS), BF), tuple(strips))
    terms = []
    for head in range(2):
        payload = call(
            functools.partial(attend_last, head),
            pay_shapes,
            (*q_pieces, *lasts[head], *states[head], *(lasts[1] if head == 0 else (strips[3], early[1]))),
            scratch=(*state_scratch, *query_scratch),
            far=2,
            **costs,
        )
        if head == 1:
            payload = hold(payload, terms[4])
        early = [payload[0]] + [swap4(payload[e], e) for e in (1, 2, 3)]
        out = call(merge, jax.ShapeDtypeStruct((ROWS, HEAD), BF), (*early, *[terms[at] for at in (1,2,3,5,6) if head == 1]), far=5 * head)
        terms += around(out)
    (mine,) = hold((mine,), terms[8])
    other = turn(mine, "c", 2, 1)
    weight = call(both, jax.ShapeDtypeStruct((8, 2 * HEAD, ROWS), BF), (mine, other))
    total = call(functools.partial(project, 0), jax.ShapeDtypeStruct((ROWS, ROWS), F32), (*terms[:8], weight))
    return call(functools.partial(project, 1), jax.ShapeDtypeStruct((ROWS, ROWS), BF), (*terms[8:], weight, total))


def solution(mesh):
    fine = Mesh(mesh.devices.reshape(8, 2, 2, 2, 4), ("z", "xl", "c", "xh", "y"))
    ctx, head = ("z", "xl", "c"), ("xh", "y")
    in_specs = (P(ctx, head), P(ctx, head), P(ctx, head), P(head, None))
    return jax.shard_map(
        local, mesh=fine, in_specs=in_specs, out_specs=P(ctx, head), check_vma=False
    )
```

```python
import functools

import jax
import jax.numpy as jnp
from jax import lax
from jax.experimental import pallas as pl
from jax.experimental.pallas import tpu as pltpu
from jax.sharding import Mesh, PartitionSpec as P

HEAD = 128
ROWS = 512
HALF = 256
REACH = 100.0
PAY = HEAD + 16
LOG2E = 1.4426950408889634
SCALE = HEAD ** (-0.5) * LOG2E
LOW = -1e30
BF = jnp.bfloat16
F32 = jnp.float32
VMEM = pl.BlockSpec(memory_space=pltpu.VMEM)
HBM = pl.BlockSpec(memory_space=pl.ANY)
ARGUMENT = pl.BlockSpec(memory_space=pltpu.HBM)
SMEM = pl.BlockSpec(memory_space=pltpu.SMEM)
PARAMS = pltpu.CompilerParams(vmem_limit_bytes=24 * 1024 * 1024)
LARGE = pltpu.CompilerParams(vmem_limit_bytes=8 * 1024 * 1024)
SMALL = pltpu.CompilerParams(vmem_limit_bytes=8 * 1024 * 1024)


def call(kernel, shapes, operands, scratch=(), flops=0, bytes_accessed=0, exps=0, smem=0, far=0, aliases=None):
    return pl.pallas_call(
        kernel,
        out_shape=shapes,
        in_specs=[SMEM] * smem + [VMEM] * (len(operands) - smem - far) + [HBM] * far,
        out_specs=jax.tree.map(lambda _: VMEM, shapes),
        scratch_shapes=scratch,
        input_output_aliases=aliases or {},
        compiler_params=PARAMS,
        cost_estimate=pl.CostEstimate(flops=flops, bytes_accessed=bytes_accessed, transcendentals=exps),
    )(*operands)


def prepare(q_far, k_far, v_far, qt_ref, kv0_ref, kv1_ref, q_ref, k_ref, v_ref, sem):
    copies = [
        pltpu.make_async_copy(far, near, sem.at[at])
        for at, (far, near) in enumerate(((q_far, q_ref), (k_far, k_ref), (v_far, v_ref)))
    ]
    for copy in copies:
        copy.start()
    for copy in copies:
        copy.wait()
    turned = q_ref[...].T
    qt_ref[...] = turned
    for head, out in ((0, kv0_ref), (1, kv1_ref)):
        columns = slice(head * HEAD, (head + 1) * HEAD)
        for half in range(2):
            at = half * ROWS
            out[at : at + HALF, :] = k_ref[half * HALF : (half + 1) * HALF, columns]
            for block in range(2):
                rows = slice(half * HALF + block * HEAD, half * HALF + (block + 1) * HEAD)
                to = at + HALF + block * HEAD
                out[to : to + HEAD, :] = v_ref[rows, columns].T


def unpack(first, second):
    keys = jnp.concatenate([first[0:HALF, :], second[0:HALF, :]], axis=0)
    blocks = [part[HALF + b * HEAD : HALF + (b + 1) * HEAD, :] for part in (first, second) for b in (0, 1)]
    return keys, jnp.concatenate(blocks, axis=1)


def spot():
    return lax.axis_index("xl") * 2 + lax.axis_index("c")


class Flash:
    def __init__(self, head, place, queries, stat_ref, acc_ref, query_ref):
        self.place, self.query_ref = place, query_ref
        for piece, query in enumerate(queries):
            query_ref[:, self.columns(piece)] = query[head * HEAD : (head + 1) * HEAD, :]
        self.stat_ref, self.acc_ref = stat_ref, acc_ref

    def columns(self, piece):
        if isinstance(piece, int):
            return slice(piece * ROWS, (piece + 1) * ROWS)
        return pl.ds(pl.multiple_of(piece * ROWS, ROWS), ROWS)

    def query(self, piece):
        return self.query_ref[:, self.columns(piece)]

    def start(self):
        width = 4 * ROWS
        self.stat_ref[0:1, :] = jnp.full((1, width), LOW, F32)
        self.stat_ref[1:2, :] = jnp.zeros((1, width), F32)
        self.acc_ref[...] = jnp.zeros(self.acc_ref.shape, F32)
        query = self.query_ref[...].astype(F32)
        self.stat_ref[2:3, :] = jnp.sqrt(jnp.sum(query * query, axis=0, keepdims=True)) * SCALE

    def score(self, piece, keys):
        return jnp.dot(keys, self.query(piece), preferred_element_type=F32) * SCALE

    def settle(self, piece, scores):
        columns = self.columns(piece)
        old = self.stat_ref[0:1, columns]
        new = jnp.maximum(old, jnp.max(scores, axis=0, keepdims=True))
        weights = jnp.exp2(scores - new)
        fade = jnp.exp2(old - new)
        self.stat_ref[0:1, columns] = new
        self.stat_ref[1:2, columns] = self.stat_ref[1:2, columns] * fade + jnp.sum(
            weights, axis=0, keepdims=True
        )
        self.acc_ref[:, columns] = self.acc_ref[:, columns] * fade
        return weights.astype(BF)

    def keep(self, piece, scores):
        columns = self.columns(piece)
        weights = jnp.exp2(scores - self.stat_ref[0:1, columns])
        self.stat_ref[1:2, columns] = self.stat_ref[1:2, columns] + jnp.sum(
            weights, axis=0, keepdims=True
        )
        return weights.astype(BF)

    def gather(self, piece, values, weights):
        columns = self.columns(piece)
        self.acc_ref[:, columns] = self.acc_ref[:, columns] + jnp.dot(
            values, weights, preferred_element_type=F32
        )

    def absorb(self, keys, values):
        following, waiting = self.score(0, keys), None
        for piece in range(4):
            scores = following
            if piece < 3:
                following = self.score(piece + 1, keys)
            if waiting is not None:
                self.gather(*waiting)
            waiting = (piece, values, self.keep(piece, scores))
        self.gather(*waiting)

    def level(self, piece, keys, values):
        self.gather(piece, values, self.settle(piece, self.score(piece, keys)))

    def full(self, keys, values):
        sizes = keys.astype(F32)
        longest = jnp.max(jnp.sum(sizes * sizes, axis=1, keepdims=True))
        reach = jnp.max(self.stat_ref[2:3, :]) ** 2 * longest
        lowest = jnp.min(self.stat_ref[0:1, :])
        room = lowest + REACH
        stays = (room > 0.0) & (reach <= room * room)

        @pl.when(stays)
        def _():
            self.absorb(keys, values)

        @pl.when(jnp.logical_not(stays))
        def _():
            @pl.loop(0, 4)
            def _(piece):
                self.level(piece, keys, values)

    def diagonal(self, keys, values):
        scores = self.score(0, keys)
        key_at = lax.broadcasted_iota(jnp.int32, scores.shape, 0)
        query_at = lax.broadcasted_iota(jnp.int32, scores.shape, 1)
        scores = jnp.where(key_at <= query_at, scores, LOW)
        self.gather(0, values, self.settle(0, scores))
        @pl.loop(1, 4)
        def _(piece):
            @pl.when((self.place ^ piece) > self.place)
            def _():
                self.level(piece, keys, values)

    def finish(self, outs):
        for piece in range(4):
            columns = self.columns(piece)
            total = self.stat_ref[1:2, columns]
            some = total > 0.0
            safe = jnp.where(some, total, 1.0)
            outs[piece][0:HEAD, :] = (self.acc_ref[:, columns] / safe).astype(BF)
            level = jnp.where(some, self.stat_ref[0:1, columns] + jnp.log2(safe), LOW)
            high = level.astype(BF)
            rest = level - high.astype(F32)
            middle = rest.astype(BF)
            low = (rest - middle.astype(F32)).astype(BF)
            row = lax.broadcasted_iota(jnp.int32, (16, ROWS), 0)
            parts = jnp.where(
                row == 0,
                high.astype(F32),
                jnp.where(row == 1, middle.astype(F32), jnp.where(row == 2, low.astype(F32), 0.0)),
            )
            outs[piece][HEAD:PAY, :] = parts.astype(BF)


def attend_first(head, q0, q1, q2, q3, own, up, down, stat_ref, acc_ref, query_ref, chunk_ref):
    plane = lax.axis_index("z")
    flash = Flash(head, spot(), (q0, q1, q2, q3), stat_ref, acc_ref, query_ref)
    flash.start()
    flash.diagonal(*unpack(own[0:ROWS, :], own[ROWS : 2 * ROWS, :]))
    either(flash, plane, 1, up, down, chunk_ref)


def either(flash, plane, distance, up, down, chunk_ref):
    @pl.loop(0, 2)
    def _(side):
        for at, active, part in ((0, plane >= distance, up), (1, plane + distance >= 8, down)):

            @pl.when(active & (side == at))
            def _():
                chunk_ref[...] = part[...]

        @pl.when(jnp.where(side == 0, plane >= distance, plane + distance >= 8))
        def _():
            flash.full(*unpack(chunk_ref[0:ROWS, :], chunk_ref[ROWS : 2 * ROWS, :]))


def attend_next(head, distance, q0, q1, q2, q3, up, down, stat_in, acc_in, stat_ref, acc_ref, query_ref, chunk_ref):
    stat_ref[...] = stat_in[...]
    acc_ref[...] = acc_in[...]
    flash = Flash(head, spot(), (q0, q1, q2, q3), stat_ref, acc_ref, query_ref)
    either(flash, lax.axis_index("z"), distance, up, down, chunk_ref)


def attend_last(head, q0, q1, q2, q3, up, down, stat_in, acc_in, *others):
    o0, o1, o2, o3, stat_ref, acc_ref, query_ref = others[-7:]
    stat_ref[...] = stat_in[...]
    acc_ref[...] = acc_in[...]
    flash = Flash(head, spot(), (q0, q1, q2, q3), stat_ref, acc_ref, query_ref)

    @pl.when(lax.axis_index("z") >= 4)
    def _():
        flash.full(*unpack(up[...], down[...]))

    flash.finish((o0, o1, o2, o3))


def merge(p0, p1, p2, p3, *others):
    out_ref = others[-1]
    pieces = (p0, p1, p2, p3)
    levels = []
    for piece in pieces:
        parts = piece[HEAD:PAY, :].astype(F32)
        levels.append(parts[0:1, :] + parts[1:2, :] + parts[2:3, :])
    top = functools.reduce(jnp.maximum, levels)
    shares = [jnp.exp2(level - top) for level in levels]
    total = functools.reduce(jnp.add, shares)
    mixed = sum(
        piece[0:HEAD, :].astype(F32) * (share / total) for piece, share in zip(pieces, shares)
    )
    out_ref[...] = mixed.T.astype(BF)


def project(head, *refs):
    parts, weight, out_ref = refs[:8], refs[8], refs[-1]
    total = refs[9][...] if len(refs) > 10 else None
    for at in range(0, 8, 2):
        left = jnp.concatenate([parts[at][...], parts[at + 1][...]], axis=1)
        rows = slice(head * HEAD, (head + 1) * HEAD)
        right = jnp.concatenate([weight[at, rows, :], weight[at + 1, rows, :]], axis=0)
        term = jnp.dot(left, right, preferred_element_type=F32)
        total = term if total is None else total + term
    out_ref[...] = total.astype(out_ref.dtype)


def hold(values, *after):
    count = len(values)
    return pl.pallas_call(
        lambda *refs: None,
        out_shape=tuple(jax.ShapeDtypeStruct(v.shape, v.dtype) for v in values),
        in_specs=[HBM] * (count + len(after)),
        out_specs=(HBM,) * count,
        input_output_aliases={i: i for i in range(count)},
        compiler_params=SMALL,
    )(*values, *after)


def turn(value, axis, size, step):
    return lax.ppermute(value, axis, [(i, (i + step) % size) for i in range(size)])


def around(own):
    return [
        part
        for half in (own, turn(own, "xh", 2, 1))
        for part in (half, turn(half, "y", 4, -1), turn(half, "y", 4, 1), turn(half, "y", 4, 2))
    ]


def cut(w_far, _, mine, other, strip, sem):
    first = lax.axis_index("c") * HEAD
    copy = pltpu.make_async_copy(w_far.at[pl.ds(pl.multiple_of(first, HEAD), HEAD), :], strip, sem)
    copy.start()
    copy.wait()
    for out, side in ((mine, lax.axis_index("xh")), (other, lax.axis_index("xh") ^ 1)):
        out[...] = strip[:, pl.ds(pl.multiple_of(side * (4 * ROWS), 4 * ROWS), 4 * ROWS)]


def split(mine, other, _, *outs):
    for out, dy in zip(outs, (0, 1, 3, 2)):
        columns = pl.ds(pl.multiple_of(((lax.axis_index("y") + 4 - dy) & 3) * ROWS, ROWS), ROWS)
        out[0:HEAD, :] = mine[:, columns]
        out[HEAD : 2 * HEAD, :] = other[:, columns]


def pile(*refs):
    for at in range(4):
        refs[4][at * 2 * HEAD : (at + 1) * 2 * HEAD, :] = refs[at][...]


def both(mine, other, weight_ref):
    here = lax.axis_index("c")
    for at in range(8):
        piece = (at % 4) * 2 * HEAD + (at // 4) * HEAD
        for index, part in ((here, mine), (1 - here, other)):
            rows = pl.ds(pl.multiple_of(index * HEAD, HEAD), HEAD)
            weight_ref[at, rows, :] = part[piece : piece + HEAD, :]


def halve(up, down, first, second):
    first[...] = up[0:ROWS, :]
    second[...] = down[ROWS : 2 * ROWS, :]


def swap4(value, e):
    return lax.ppermute(value, ("xl", "c"), [(i, i ^ e) for i in range(4)])


def local(queries, keys, values, w_out):
    qt, kv0, kv1 = pl.pallas_call(
        prepare,
        out_shape=(
            jax.ShapeDtypeStruct((2 * HEAD, ROWS), BF),
            jax.ShapeDtypeStruct((2 * ROWS, HEAD), BF),
            jax.ShapeDtypeStruct((2 * ROWS, HEAD), BF),
        ),
        in_specs=[ARGUMENT] * 3,
        out_specs=(VMEM,) * 3,
        scratch_shapes=(*[pltpu.VMEM((ROWS, 2 * HEAD), BF)] * 3, pltpu.SemaphoreType.DMA((3,))),
        compiler_params=LARGE,
        cost_estimate=pl.CostEstimate(flops=2**36, bytes_accessed=0, transcendentals=0),
    )(queries, keys, values)
    state_shapes = (jax.ShapeDtypeStruct((8, 4 * ROWS), F32), jax.ShapeDtypeStruct((HEAD, 4 * ROWS), F32))
    state_scratch = (pltpu.VMEM((8, 4 * ROWS), F32), pltpu.VMEM((HEAD, 4 * ROWS), F32))
    pay_shapes = tuple(jax.ShapeDtypeStruct((PAY, ROWS), BF) for _ in range(4))
    query_scratch = (pltpu.VMEM((HEAD, 4 * ROWS), BF),)
    chunk_scratch = (*query_scratch, pltpu.VMEM((2 * ROWS, HEAD), BF))
    costs = dict(flops=4 * 2**30, bytes_accessed=4 * 2**21, exps=0)

    own = [kv0, kv1]
    ups, downs = [turn(kv0, "z", 8, 1)], [turn(kv0, "z", 8, -1)]
    q_cross, q_core = turn(qt, "xl", 2, 1), turn(qt, "c", 2, 1)
    (q_cross,) = hold((q_cross,), ups[0], downs[0])
    ups.append(turn(own[1], "z", 8, 1))
    downs.append(turn(own[1], "z", 8, -1))
    q_pieces = [qt, q_core, q_cross, turn(q_cross, "c", 2, 1)]

    mine, other = pl.pallas_call(
        cut,
        out_shape=(jax.ShapeDtypeStruct((HEAD, 4 * ROWS), BF),) * 2,
        in_specs=[ARGUMENT, HBM],
        out_specs=(VMEM,) * 2,
        scratch_shapes=(pltpu.VMEM((HEAD, 8 * ROWS), BF), pltpu.SemaphoreType.DMA),
        compiler_params=SMALL,
    )(w_out, q_pieces[3])
    other = turn(other, "xh", 2, 1)

    states = [
        call(
            functools.partial(attend_first, head),
            state_shapes,
            (*q_pieces, own[head], ups[head], downs[head]),
            scratch=chunk_scratch,
            **costs,
        )
        for head in range(2)
    ]
    strips = list(call(split, (jax.ShapeDtypeStruct((2 * HEAD, ROWS), BF),) * 4, (mine, other, states[0][0]), far=1))
    strips[1] = turn(strips[1], "y", 4, -1)
    for at, dy in ((2, -1), (3, 2)):
        (held,) = hold((strips[at],), strips[at - 1])
        strips[at] = turn(held, "y", 4, -dy)
    before = {(2, 1): (other,), (3, 1): strips[1:2]}
    for distance in (2, 3):
        for head in range(2):
            up, down = turn(ups[head], "z", 8, 1), turn(downs[head], "z", 8, -1)
            ups[head], downs[head] = hold((up, down), states[head][0], *before.get((distance, head), ()))
            states[head] = call(
                functools.partial(attend_next, head, distance),
                state_shapes,
                (*q_pieces, ups[head], downs[head], *states[head]),
                scratch=chunk_scratch,
                aliases={6: 0, 7: 1},
                **costs,
            )
    lasts = []
    for head in range(2):
        halves = call(halve, (jax.ShapeDtypeStruct((ROWS, HEAD), BF),) * 2, (ups[head], downs[head]))
        lasts.append((turn(halves[0], "z", 8, 1), turn(halves[1], "z", 8, -1)))
    mine = call(pile, jax.ShapeDtypeStruct((8 * HEAD, ROWS), BF), tuple(strips))
    terms = []
    for head in range(2):
        payload = call(
            functools.partial(attend_last, head),
            pay_shapes,
            (*q_pieces, *lasts[head], *states[head], *(lasts[1] if head == 0 else (strips[3], early[1]))),
            scratch=(*state_scratch, *query_scratch),
            far=2,
            **costs,
        )
        if head == 1:
            payload = hold(payload, terms[4])
        early = [payload[0]] + [swap4(payload[e], e) for e in (1, 2, 3)]
        out = call(merge, jax.ShapeDtypeStruct((ROWS, HEAD), BF), (*early, *[terms[at] for at in (1, 2, 3, 5) if head == 1]), far=4 * head)
        terms += around(out)
    (mine,) = hold((mine,), terms[8])
    other = turn(mine, "c", 2, 1)
    weight = call(both, jax.ShapeDtypeStruct((8, 2 * HEAD, ROWS), BF), (mine, other))
    total = call(functools.partial(project, 0), jax.ShapeDtypeStruct((ROWS, ROWS), F32), (*terms[:8], weight))
    return call(functools.partial(project, 1), jax.ShapeDtypeStruct((ROWS, ROWS), BF), (*terms[8:], weight, total))


def solution(mesh):
    fine = Mesh(mesh.devices.reshape(8, 2, 2, 2, 4), ("z", "xl", "c", "xh", "y"))
    ctx, head = ("z", "xl", "c"), ("xh", "y")
    in_specs = (P(ctx, head), P(ctx, head), P(ctx, head), P(head, None))
    return jax.shard_map(
        local, mesh=fine, in_specs=in_specs, out_specs=P(ctx, head), check_vma=False
    )
```
